512 devices in a mesh: dp: 4 (over y_hi, core), ctx: 128 (over y_lo, z, x).
Axes of the slice: x: 4, y: 4 (y_hi: 2, y_lo: 2; y = y_hi * 2 + y_lo), z: 16, core: 2. Of those that a mesh axis runs over, the one named last changes fastest.
Arguments:
- queries: bfloat16 [4, 32768, 768], P('dp', 'ctx'), may hold values from -12 to 12
- key_rows: bfloat16 [4, 32768, 768], P('dp', 'ctx'), may hold values from -6 to 6
- value_rows: bfloat16 [4, 32768, 768], P('dp', 'ctx'), may hold values from -6 to 6
- out_weight: bfloat16 [768, 768], P('ctx'), may hold values from -0.21875 to 0.21875
- cotangent: bfloat16 [4, 32768, 768], P('dp', 'ctx'), may hold values from -24 to 24
Outputs:
- grad_queries: bfloat16 [4, 32768, 768], P('dp', 'ctx')
- grad_keys: bfloat16 [4, 32768, 768], P('dp', 'ctx')
- grad_values: bfloat16 [4, 32768, 768], P('dp', 'ctx')
- grad_weight: float32 [768, 768], P('ctx')
The draws below stay inside these ranges and needn't reach their ends.
All inputs are finite; a program needn't handle non-finite values.
Results may differ from the reference program's by a relative error of at most 0.025.
Values may be sent and summed in bfloat16 or wider, within the bound.
A program may use at most 64 MiB of HBM per device.

```python
from functools import partial
import jax
import jax.numpy as jnp
from jax import lax

HS = 96
HR = 4
HC = 4
DOUT = 768
STRIDE = 1024
BATCH = 4
TOKENS = 32768
F = 768


def draw_queries(key, part):
    key = jax.random.fold_in(key, 1)
    values = jnp.clip(jax.random.normal(key, (BATCH, TOKENS, F)), -6.0, 6.0)
    return values.astype(jnp.bfloat16)


def draw_key_rows(key, part):
    key = jax.random.fold_in(key, 2)
    values = jnp.clip(jax.random.normal(key, (BATCH, TOKENS, F)), -6.0, 6.0)
    return values.astype(jnp.bfloat16)


def raised(result, key, source, target, blocks, factor):
    def block_of(axis_at):
        return (jnp.arange(result.shape[axis_at]) // (result.shape[axis_at] // blocks)).reshape((-1,) + (1,) * (result.ndim - 1 - axis_at))

    first = jax.random.permutation(key, blocks)[block_of(target)]
    other_side = (block_of(target) + blocks // 2) % blocks
    return jnp.where((block_of(source) == first) | (block_of(source) == other_side), factor * result, result)


def shard_levels(key, shape, pieces, smallest, largest):
    def one(position, blocks):
        heights = jax.random.uniform(jax.random.fold_in(jax.random.fold_in(key, 6), position), (blocks,), jnp.float32, smallest / len(pieces), largest / len(pieces))
        return jnp.repeat(jnp.exp(heights), shape[position] // blocks).reshape((-1,) + (1,) * (len(shape) - position - 1))

    level = one(*pieces[0])
    for cut in pieces[1:]:
        level = level * one(*cut)
    return level


def centred(key, dims, width, bound, split=(), held_as=jnp.bfloat16):
    factor_of = shard_levels(key, dims, split, -0.22, 0.18) if split else 1.0
    result = jax.random.normal(key, dims, jnp.float32) * width * factor_of
    return jnp.minimum(jnp.maximum(result, -bound), bound).astype(held_as)


def bell_draw_with(own_key, dims, scale, reach, split, heavy, kind=jnp.bfloat16):
    entries = scale * jax.random.normal(own_key, dims, jnp.float32)
    if split:
        entries = entries * shard_levels(own_key, dims, split, -0.22, 0.18)
    return jnp.clip(raised(entries, jax.random.fold_in(own_key, 3), *heavy), -reach, reach).astype(kind)


def setup_inputs(seed: int = 0) -> dict:
    arg_keys = jax.random.split(jax.random.key(seed), 6)
    queries = draw_queries(jax.random.fold_in(arg_keys[5], 71), 0)
    key_rows = draw_key_rows(jax.random.fold_in(arg_keys[5], 71), 0)
    value_rows = centred(arg_keys[2], (BATCH, TOKENS, F), 1.0, 6.0, ((0, 4), (1, 128)))
    out_weight = centred(arg_keys[3], (DOUT, F), DOUT ** -0.5, 0.21875, ((0, 128),))
    cotangent = bell_draw_with(arg_keys[4], (BATCH, TOKENS, DOUT), 1.0, 24.0, ((0, 4), (1, 128)), (1, 2, 128, 5.5))
    return {"queries": queries, "key_rows": key_rows, "value_rows": value_rows, "out_weight": out_weight, "cotangent": cotangent}


def head_grads(query_heads, key_heads, value_heads, out_heads, allowed):
    score_scale = HS ** -0.5
    scores = jnp.einsum("qhd,khd->hqk", query_heads.astype(jnp.float32), key_heads.astype(jnp.float32)) * score_scale
    scores = jnp.where(allowed[None], scores, -1e30)
    row_max = jnp.max(scores, axis=-1, keepdims=True)
    log_total = row_max + jnp.log(jnp.sum(jnp.exp(scores - row_max), axis=-1, keepdims=True))
    probs = jnp.exp(scores - log_total)
    probs_half = probs.astype(jnp.bfloat16)
    attended = jnp.einsum("hqk,khd->qhd", probs_half.astype(jnp.float32), value_heads.astype(jnp.float32)).astype(jnp.bfloat16)
    deltas = jnp.sum(out_heads.astype(jnp.float32) * attended.astype(jnp.float32), axis=-1).T
    dprobs = jnp.einsum("qhd,khd->hqk", out_heads.astype(jnp.float32), value_heads.astype(jnp.float32))
    dscores = (probs * (dprobs - deltas[:, :, None]) * score_scale).astype(jnp.bfloat16)
    grad_query = jnp.einsum("hqk,khd->qhd", dscores.astype(jnp.float32), key_heads.astype(jnp.float32))
    grad_key = jnp.einsum("hqk,qhd->khd", dscores.astype(jnp.float32), query_heads.astype(jnp.float32))
    grad_value = jnp.einsum("hqk,qhd->khd", probs_half.astype(jnp.float32), out_heads.astype(jnp.float32))
    return attended, grad_query.astype(jnp.bfloat16), grad_key.astype(jnp.bfloat16), grad_value.astype(jnp.bfloat16)


def reference(queries, key_rows, value_rows, out_weight, cotangent):
    row_width = HR * HS
    blocks_count = TOKENS // STRIDE
    grad_out = jnp.dot(cotangent.reshape(BATCH * TOKENS, DOUT), out_weight, preferred_element_type=jnp.float32)
    grad_out = grad_out.astype(jnp.bfloat16).reshape(BATCH, TOKENS, F)
    inputs = (queries, key_rows, value_rows, grad_out)

    def to_blocks(array):
        return array[:, :, :row_width].reshape(BATCH * blocks_count, STRIDE, HR, HS)

    causal_rows = jnp.tril(jnp.ones((STRIDE, STRIDE), dtype=bool))

    def row_block(parts):
        return head_grads(parts[0], parts[1], parts[2], parts[3], causal_rows)

    row_out = lax.map(row_block, tuple(to_blocks(array) for array in inputs))
    row_out = [array.reshape(BATCH, TOKENS, row_width) for array in row_out]

    def to_classes(array):
        shaped = array[:, :, row_width:].reshape(BATCH, blocks_count, STRIDE, HC, HS)
        return shaped.transpose(0, 2, 1, 3, 4).reshape(BATCH * STRIDE, blocks_count, HC, HS)

    def to_tokens(array):
        shaped = array.reshape(BATCH, STRIDE, blocks_count, HC, HS)
        return shaped.transpose(0, 2, 1, 3, 4).reshape(BATCH, TOKENS, HC * HS)

    causal_blocks = jnp.tril(jnp.ones((blocks_count, blocks_count), dtype=bool))
    column_out = jax.vmap(partial(head_grads, allowed=causal_blocks))(
        to_classes(queries), to_classes(key_rows), to_classes(value_rows), to_classes(grad_out))
    merged = [jnp.concatenate([row_out[index], to_tokens(column_out[index])], axis=2) for index in range(4)]
    grad_weight = jnp.dot(cotangent.reshape(BATCH * TOKENS, DOUT).T, merged[0].reshape(BATCH * TOKENS, F),
                          preferred_element_type=jnp.float32)
    return (merged[1], merged[2], merged[3], grad_weight)
```

```python
import jax
import jax.numpy as jnp
import numpy as np
from jax import lax
from jax.experimental import pallas as pl
from jax.experimental.pallas import tpu as pltpu
from jax.sharding import PartitionSpec as P

HS = 96
HEADS = 4
WIDTH = HEADS * HS
NX, NZ = 4, 16
GROUP = 32
ROWS = 256
CLASSES = 8
SCALE = HS**-0.5
F32, BF16 = jnp.float32, jnp.bfloat16
NT = (((1,), (1,)), ((), ()))
TN = (((0,), (0,)), ((), ()))


def dot(a, b, dims=None):
    if dims is None:
        return jnp.dot(a, b, preferred_element_type=F32)
    return lax.dot_general(a, b, dims, preferred_element_type=F32)


def selections():
    spread = np.zeros((768, 1024), np.float32)
    gather = np.zeros((1024, 768), np.float32)
    for yl in range(2):
        for z in range(NZ):
            for x in range(NX):
                for r in range(6):
                    f = (yl * 64 + z * 4 + x) * 6 + r
                    spread[f, ((yl * 4 + x) * 16 + z) * 8 + r] = 1
                    gather[(((z // 8 * 4 + x) * 2 + yl) * 8 + z % 8) * 8 + r, f] = 1
    pad = np.zeros((WIDTH, 512), np.float32)
    for h in range(HEADS):
        for i in range(HS):
            pad[h * HS + i, h * 128 + i] = 1
    return [jnp.asarray(m, BF16) for m in (spread, gather, pad, pad.T)]


def kernel(
    q_ref, k_ref, v_ref, w_ref, c_ref, spread_ref, gather_ref, pad_ref, unpad_ref,
    gq_ref, gk_ref, gv_ref, gw_ref,
    wz_send, wz_recv, wg, cot_p, cot_t, go,
    cs, cr, qc, kc, vc, dc, probs_ref, half_ref, ds_ref, acc0, acc1,
    rs, rr, rs_do, rr_do, rt_s, rt_r, racc_k, racc_v, att_ref,
    g1_s, g1_r, g_own, g2_s, g2_r, g3_s, g3_r, g4_s, g4_r, g5_s, g5_r,
    ssem, rsem,
):
    dp, ctx = lax.axis_index("dp"), lax.axis_index("ctx")
    core, yh = dp % 2, dp // 2
    x, p = ctx % 4, ctx // 4
    z, yl = p % 16, p // 16
    y = yh * 2 + yl

    def at_p(pp):
        return (dp, pp * 4 + x)

    def at_x(xx):
        return (dp, p * 4 + xx)

    def at_y(yy):
        return ((yy // 2) * 2 + core, (yy % 2) * 64 + z * 4 + x)

    def at_core():
        return (yh * 2 + 1 - core, ctx)

    def send(src, dst, sem, where):
        pltpu.make_async_remote_copy(
            src_ref=src, dst_ref=dst, send_sem=ssem.at[sem], recv_sem=rsem.at[sem],
            device_id=where, device_id_type=pl.DeviceIdType.MESH,
        ).start()

    def take(ref, sem):
        pltpu.make_async_copy(ref, ref, rsem.at[sem]).wait()

    def sent(ref, sem):
        pltpu.make_async_copy(ref, ref, ssem.at[sem]).wait()

    barrier = pltpu.get_barrier_semaphore()

    def greet(where):
        pl.semaphore_signal(barrier, inc=1, device_id=where, device_id_type=pl.DeviceIdType.MESH)

    def greet_p(i, _):
        greet(at_p((p + i) % GROUP))
        return 0

    lax.fori_loop(1, GROUP, greet_p, 0)
    for i in range(1, 4):
        greet(at_x((x + i) % 4))
        greet(at_y((y + i) % 4))
    greet(at_core())
    greet(((1 - yh) * 2 + 1 - core, ctx))

    def pack(slot, a_ref, a0, b_ref, b0):
        def one(m, _):
            rows = pl.ds(pl.multiple_of(m * 16, 16), 16)
            a = a_ref[rows, a0 : a0 + WIDTH].astype(F32)
            b = b_ref[rows, b0 : b0 + WIDTH].astype(F32)
            cs[slot, 2 * m] = jnp.concatenate([a[:8], b[:8]], 0).astype(BF16)
            cs[slot, 2 * m + 1] = jnp.concatenate([a[8:], b[8:]], 0).astype(BF16)
            return 0

        lax.fori_loop(0, 16, one, 0)

    def exchange(slot):
        def one(i, _):
            half = (i + 1) // 2
            ahead = (i % 2) * half + (1 - i % 2) * (GROUP - half)
            pp = (p + ahead) % GROUP
            send(cs.at[slot, pp], cr.at[slot, p], slot, at_p(pp))
            return 0

        lax.fori_loop(1, GROUP, one, 0)
        cr[slot, p] = cs[slot, p]

    def arrived(slot):
        take(cr.at[slot, pl.ds(0, GROUP - 1)], slot)

    def unpack(slot, a_ref, a0, b_ref, b0):
        def one(m, _):
            rows = pl.ds(pl.multiple_of(m * 16, 16), 16)
            first = cr[slot, 2 * m].astype(F32)
            second = cr[slot, 2 * m + 1].astype(F32)
            a_ref[rows, a0 : a0 + WIDTH] = jnp.concatenate([first[:8], second[:8]], 0).astype(BF16)
            b_ref[rows, b0 : b0 + WIDTH] = jnp.concatenate([first[8:], second[8:]], 0).astype(BF16)
            return 0

        lax.fori_loop(0, 16, one, 0)

    w = w_ref[...].astype(F32)
    wz_send[...] = jnp.zeros((8, WIDTH), F32)
    wz_send[0:6, :] = jnp.where(core == 0, w[:, :WIDTH], w[:, WIDTH:])
    wz_recv[z] = wz_send[...]
    pack(0, q_ref, WIDTH, k_ref, WIDTH)
    pl.semaphore_wait(barrier, 39)

    def send_w(i, _):
        zz = (z + i) % NZ
        send(wz_send, wz_recv.at[z], 4, at_p(yl * 16 + zz))
        return 0

    lax.fori_loop(1, NZ, send_w, 0)
    exchange(0)

    for index, ref in enumerate((q_ref, k_ref, v_ref)):
        padded = dot(ref[:, :WIDTH], pad_ref[...]).astype(BF16)
        for h in range(HEADS):
            rs[h, index] = padded[:, h * 128 : (h + 1) * 128]
    for i in range(1, 4):
        xx = (x + i) % 4
        send(rs.at[xx], rr.at[x], 5, at_x(xx))
    rr[x] = rs[x]

    cot_p[...] = dot(c_ref[...], spread_ref[...]).astype(BF16)
    cot_t[...] = dot(gather_ref[...], c_ref[...], NT).astype(BF16)

    take(wz_recv.at[pl.ds(0, NZ - 1)], 4)
    wg[core, yl * 4 + x] = wz_recv[...].reshape(128, WIDTH).astype(BF16)
    own = wg.at[core, yl * 4 + x]
    for i in range(1, 4):
        send(own, own, 6, at_x((x + i) % 4))
    mine = wg.at[core, pl.ds(yl * 4, 4)]
    take(wg.at[core, pl.ds(yl * 4, 3)], 6)
    for i, first in ((1, 0), (3, 2)):
        part = wg.at[core, pl.ds(yl * 4 + first, 2)]
        send(part, part, 7, at_y((y + i) % 4))
    send(mine, mine, 8, at_core())
    other = wg.at[core, pl.ds((1 - yl) * 4, 4)]
    take(other, 7)
    send(other, other, 9, at_core())
    take(wg.at[1 - core, pl.ds(yl * 4, 4)], 8)
    take(wg.at[1 - core, pl.ds((1 - yl) * 4, 4)], 9)
    for c in range(2):
        go[:, c * WIDTH : (c + 1) * WIDTH] = dot(
            cot_p[...], wg[c].reshape(1024, WIDTH)
        ).astype(BF16)

    pack(1, v_ref, WIDTH, go, WIDTH)
    exchange(1)
    padded = dot(go[:, :WIDTH], pad_ref[...]).astype(BF16)
    for h in range(HEADS):
        rs_do[h] = padded[:, h * 128 : (h + 1) * 128]
    for i in range(1, 4):
        xx = (x + i) % 4
        send(rs_do.at[xx], rr_do.at[x], 10, at_x(xx))
    rr_do[x] = rs_do[x]

    arrived(0)
    unpack(0, qc, 0, kc, 0)
    row_at = lax.broadcasted_iota(jnp.int32, (ROWS, ROWS), 0)
    key_at = lax.broadcasted_iota(jnp.int32, (ROWS, ROWS), 1)
    lanes = lax.broadcasted_iota(jnp.int32, (ROWS, WIDTH), 1)

    def span(h):
        return h * HS // 128 * 128, -(-(h + 1) * HS // 128) * 128

    def head(ref, h):
        lo, hi = span(h)
        at = lanes[:, lo:hi]
        value = ref[:, lo:hi]
        return jnp.where((at >= h * HS) & (at < (h + 1) * HS), value, jnp.zeros_like(value))

    def softmax(scores):
        top = jnp.max(scores, axis=1, keepdims=True)
        total = top + jnp.log(jnp.sum(jnp.exp(scores - top), axis=1, keepdims=True))
        return jnp.exp(scores - total)

    for h in range(HEADS):
        lo, hi = span(h)
        scores = dot(head(qc, h), kc[:, lo:hi], NT) * SCALE
        allowed = (key_at <= row_at) & ((row_at - key_at) % CLASSES == 0)
        probs = softmax(jnp.where(allowed, scores, -1e30))
        probs_ref[h] = probs
        half_ref[h] = probs.astype(BF16)

    take(rr.at[pl.ds(0, 3)], 5)
    take(rr_do.at[pl.ds(0, 3)], 10)
    racc_k[...] = jnp.zeros_like(racc_k)
    racc_v[...] = jnp.zeros_like(racc_v)
    for i in range(4):
        n = (i + 1) * ROWS
        query, out = rr[i, 0], rr_do[i]
        keys = rr[0 : i + 1, 1].reshape(n, 128)
        values = rr[0 : i + 1, 2].reshape(n, 128)
        at = lax.broadcasted_iota(jnp.int32, (ROWS, n), 0) + i * ROWS
        allowed = lax.broadcasted_iota(jnp.int32, (ROWS, n), 1) <= at
        probs = softmax(jnp.where(allowed, dot(query, keys, NT) * SCALE, -1e30))
        half = probs.astype(BF16)
        attended = dot(half, values).astype(BF16)
        deltas = jnp.sum(out.astype(F32) * attended.astype(F32), axis=1, keepdims=True)
        dscores = (probs * (dot(out, values, NT) - deltas) * SCALE).astype(BF16)
        rt_s[i, 0] = attended
        rt_s[i, 1] = dot(dscores, keys).astype(BF16)
        racc_k[0:n, :] += dot(dscores, query, TN)
        racc_v[0:n, :] += dot(half, out, TN)
    for i in range(4):
        rt_s[i, 2] = racc_k[i * ROWS : (i + 1) * ROWS, :].astype(BF16)
        rt_s[i, 3] = racc_v[i * ROWS : (i + 1) * ROWS, :].astype(BF16)
    for i in range(1, 4):
        xx = (x + i) % 4
        send(rt_s.at[xx], rt_r.at[x], 11, at_x(xx))
    rt_r[x] = rt_s[x]

    arrived(1)
    unpack(1, vc, 0, dc, 0)
    acc0[...] = jnp.zeros_like(acc0)
    acc1[...] = jnp.zeros_like(acc1)
    for h in range(HEADS):
        lo, hi = span(h)
        out = head(dc, h)
        attended = dot(half_ref[h], head(vc, h))
        acc0[:, lo:hi] += attended
        deltas = jnp.sum(out.astype(F32) * attended.astype(BF16).astype(F32), axis=1, keepdims=True)
        dprobs = dot(out, vc[:, lo:hi], NT)
        dscores = (probs_ref[h] * (dprobs - deltas) * SCALE).astype(BF16)
        ds_ref[h] = dscores
        acc1[:, lo:hi] += dot(dscores, head(kc, h))
    pack(2, acc0, 0, acc1, 0)
    exchange(2)
    acc0[...] = jnp.zeros_like(acc0)
    acc1[...] = jnp.zeros_like(acc1)
    for h in range(HEADS):
        lo, hi = span(h)
        acc0[:, lo:hi] += dot(ds_ref[h], head(qc, h), TN)
        acc1[:, lo:hi] += dot(half_ref[h], head(dc, h), TN)
    pack(3, acc0, 0, acc1, 0)
    exchange(3)

    def reduce_core(g):
        attended = att_ref[:, g * WIDTH : (g + 1) * WIDTH]
        theirs = pl.ds(pl.multiple_of((1 - core) * 512, 512), 512)
        ours = pl.ds(pl.multiple_of(core * 512, 512), 512)
        g1_s[g] = dot(cot_t[theirs, :], attended).astype(BF16)
        send(g1_s.at[g], g1_r.at[g], 12 + g, at_core())
        g_own[g] = dot(cot_t[ours, :], attended).reshape(4, 128, WIDTH)

    def reduce_x(g):
        take(g1_r.at[g], 12 + g)
        total = g_own[g] + g1_r[g].astype(F32).reshape(4, 128, WIDTH)
        g_own[g] = total
        g2_s[g] = total.astype(BF16)
        for i in range(1, 4):
            xx = (x + i) % 4
            send(g2_s.at[g, xx], g2_r.at[g, i - 1], 14 + g, at_x(xx))

    def reduce_y(g):
        take(g2_r.at[g], 14 + g)
        total = g_own[g, x]
        for i in range(3):
            total = total + g2_r[g, i].astype(F32)
        g3_s[g] = total.reshape(4, 32, WIDTH)
        for i in range(1, 4):
            yy = (y + i) % 4
            send(g3_s.at[g, (yy % 2) * 2 + yy // 2], g3_r.at[g, i - 1], 16 + g, at_y(yy))

    def reduce_z(g):
        take(g3_r.at[g], 16 + g)
        total = g3_s[g, yl * 2 + yh]
        for i in range(3):
            total = total + g3_r[g, i]
        g4_s[g] = total.reshape(4, 8, WIDTH)
        for i in range(4):
            zz = core * 8 + yh * 4 + i

            @pl.when(zz != z)
            def _():
                send(g4_s.at[g, i], g4_r.at[g, z], 18 + g, at_p(yl * 16 + zz))

    owner = (z // 8 == core) & (z // 4 % 2 == yh)

    def reduce_last(g):
        @pl.when(owner)
        def _():
            take(g4_r.at[g, pl.ds(0, NZ - 1)], 18 + g)
            g4_r[g, z] = g4_s[g, z % 4]
            g5_s[g] = jnp.sum(g4_r[g], axis=0)
            for c in (1, 2, 3):
                send(g5_s.at[g], g5_r.at[g], 20 + g, ((dp + c) % 4, ctx))

    def finish(g):
        @pl.when(owner)
        def _():
            gw_ref[:, g * WIDTH : (g + 1) * WIDTH] = g5_s[g, 0:6, :]

        @pl.when(jnp.logical_not(owner))
        def _():
            take(g5_r.at[g], 20 + g)
            gw_ref[:, g * WIDTH : (g + 1) * WIDTH] = g5_r[g, 0:6, :]

    take(rt_r.at[pl.ds(0, 3)], 11)
    for index, ref in enumerate((att_ref, gq_ref, gk_ref, gv_ref)):
        heads = jnp.concatenate([rt_r[h, index] for h in range(HEADS)], axis=1)
        ref[:, :WIDTH] = dot(heads, unpad_ref[...]).astype(BF16)
    reduce_core(0)
    reduce_x(0)
    reduce_y(0)
    arrived(2)
    unpack(2, att_ref, WIDTH, gq_ref, WIDTH)
    reduce_core(1)
    reduce_z(0)
    reduce_x(1)
    reduce_y(1)
    reduce_last(0)
    reduce_z(1)
    arrived(3)
    unpack(3, gk_ref, WIDTH, gv_ref, WIDTH)
    reduce_last(1)
    finish(0)
    finish(1)

    for slot in range(4):
        sent(cs.at[slot, pl.ds(0, GROUP - 1)], slot)
    sent(wz_recv.at[pl.ds(0, NZ - 1)], 4)
    sent(rs.at[pl.ds(0, 3)], 5)
    sent(wg.at[core, pl.ds(0, 3)], 6)
    sent(mine, 7)
    sent(mine, 8)
    sent(other, 9)
    sent(rs_do.at[pl.ds(0, 3)], 10)
    sent(rt_s.at[pl.ds(0, 3)], 11)
    for g in range(2):
        sent(g1_s.at[g], 12 + g)
        sent(g2_s.at[g, pl.ds(0, 3)], 14 + g)
        sent(g3_s.at[g, pl.ds(0, 3)], 16 + g)
        quarter = (z // 8 == core) & (z // 4 % 2 == yh)

        @pl.when(quarter)
        def _():
            sent(g4_s.at[g, pl.ds(0, 3)], 18 + g)
            sent(g4_s.at[g, pl.ds(0, 3)], 20 + g)

        @pl.when(jnp.logical_not(quarter))
        def _():
            sent(g4_s.at[g], 18 + g)


def body(queries, key_rows, value_rows, out_weight, cotangent, *matrices):
    vmem = pl.BlockSpec(memory_space=pltpu.VMEM)
    tokens = jax.ShapeDtypeStruct((ROWS, 2 * WIDTH), BF16)
    outs = pl.pallas_call(
        kernel,
        out_shape=(tokens, tokens, tokens, jax.ShapeDtypeStruct((6, 2 * WIDTH), F32)),
        in_specs=[vmem] * 9,
        out_specs=(vmem,) * 4,
        scratch_shapes=[
            pltpu.VMEM((8, WIDTH), F32),
            pltpu.VMEM((NZ, 8, WIDTH), F32),
            pltpu.VMEM((2, 8, 128, WIDTH), BF16),
            pltpu.VMEM((ROWS, 1024), BF16),
            pltpu.VMEM((1024, ROWS), BF16),
            pltpu.VMEM((ROWS, 2 * WIDTH), BF16),
            pltpu.VMEM((4, GROUP, 16, WIDTH), BF16),
            pltpu.VMEM((4, GROUP, 16, WIDTH), BF16),
            pltpu.VMEM((ROWS, WIDTH), BF16),
            pltpu.VMEM((ROWS, WIDTH), BF16),
            pltpu.VMEM((ROWS, WIDTH), BF16),
            pltpu.VMEM((ROWS, WIDTH), BF16),
            pltpu.VMEM((HEADS, ROWS, ROWS), F32),
            pltpu.VMEM((HEADS, ROWS, ROWS), BF16),
            pltpu.VMEM((HEADS, ROWS, ROWS), BF16),
            pltpu.VMEM((ROWS, WIDTH), F32),
            pltpu.VMEM((ROWS, WIDTH), F32),
            pltpu.VMEM((4, 3, ROWS, 128), BF16),
            pltpu.VMEM((4, 3, ROWS, 128), BF16),
            pltpu.VMEM((4, ROWS, 128), BF16),
            pltpu.VMEM((4, ROWS, 128), BF16),
            pltpu.VMEM((4, 4, ROWS, 128), BF16),
            pltpu.VMEM((4, 4, ROWS, 128), BF16),
            pltpu.VMEM((1024, 128), F32),
            pltpu.VMEM((1024, 128), F32),
            pltpu.VMEM((ROWS, 2 * WIDTH), BF16),
            pltpu.VMEM((2, 512, WIDTH), BF16),
            pltpu.VMEM((2, 512, WIDTH), BF16),
            pltpu.VMEM((2, 4, 128, WIDTH), F32),
            pltpu.VMEM((2, 4, 128, WIDTH), BF16),
            pltpu.VMEM((2, 3, 128, WIDTH), BF16),
            pltpu.VMEM((2, 4, 32, WIDTH), F32),
            pltpu.VMEM((2, 3, 32, WIDTH), F32),
            pltpu.VMEM((2, 4, 8, WIDTH), F32),
            pltpu.VMEM((2, NZ, 8, WIDTH), F32),
            pltpu.VMEM((2, 8, WIDTH), F32),
            pltpu.VMEM((2, 8, WIDTH), F32),
            pltpu.SemaphoreType.DMA((22,)),
            pltpu.SemaphoreType.DMA((22,)),
        ],
        compiler_params=pltpu.CompilerParams(
            collective_id=0, has_side_effects=True, vmem_limit_bytes=56 * 1024 * 1024
        ),
        cost_estimate=pl.CostEstimate(
            flops=8_000_000_000, bytes_accessed=8_000_000, transcendentals=2_000_000
        ),
        name="strided_attention",
    )(queries[0], key_rows[0], value_rows[0], out_weight, cotangent[0], *matrices)
    return (outs[0][None], outs[1][None], outs[2][None], outs[3])


def solution(mesh):
    tokens, rows = P("dp", "ctx", None), P("ctx", None)
    matrices = selections()
    mapped = jax.shard_map(
        body,
        mesh=mesh,
        in_specs=(tokens, tokens, tokens, rows, tokens) + (P(None, None),) * len(matrices),
        out_specs=(tokens, tokens, tokens, rows),
        check_vma=False,
    )

    def run(queries, key_rows, value_rows, out_weight, cotangent):
        return mapped(queries, key_rows, value_rows, out_weight, cotangent, *matrices)

    return run
```

```python
import jax
import jax.numpy as jnp
import numpy as np
from jax import lax
from jax.experimental import pallas as pl
from jax.experimental.pallas import tpu as pltpu
from jax.sharding import PartitionSpec as P

HS = 96
HEADS = 4
WIDTH = HEADS * HS
NX, NZ = 4, 16
GROUP = 32
ROWS = 256
CLASSES = 8
SCALE = HS**-0.5
F32, BF16 = jnp.float32, jnp.bfloat16
NT = (((1,), (1,)), ((), ()))
TN = (((0,), (0,)), ((), ()))


def dot(a, b, dims=None):
    if dims is None:
        return jnp.dot(a, b, preferred_element_type=F32)
    return lax.dot_general(a, b, dims, preferred_element_type=F32)


def selections():
    spread = np.zeros((768, 768), np.float32)
    gather = np.zeros((1024, 768), np.float32)
    for yl in range(2):
        for z in range(NZ):
            for x in range(NX):
                for r in range(6):
                    f = (yl * 64 + z * 4 + x) * 6 + r
                    spread[f, (((r // 3 * 2 + yl) * 4 + x) * 16 + z) * 3 + r % 3] = 1
                    gather[(((z // 8 * 4 + x) * 2 + yl) * 8 + z % 8) * 8 + r, f] = 1
    rows = np.zeros((3, 48, 256), np.float32)
    for t in range(3):
        for z in range(NZ):
            for r in range(3):
                rows[t, z * 3 + r, z * 16 + r * 3 + t] = 1
    pad = np.zeros((WIDTH, 512), np.float32)
    for h in range(HEADS):
        for i in range(HS):
            pad[h * HS + i, h * 128 + i] = 1
    return [jnp.asarray(m, BF16) for m in (spread, gather, rows, pad, pad.T)]


WZ, WX, WY, WC, RQ, RD, RT, G1, G2, G3, G4, G5 = 7, 8, 9, 12, 16, 17, 18, 19, 21, 23, 25, 27
SEMS = 29
TILES = (3, 2, 1, 1, 1, 2, 2)


def kernel(
    q_hbm, k_hbm, v_hbm, w_hbm, c_hbm, spread_hbm, gather_hbm, rows_hbm, pad_hbm, unpad_hbm,
    gq_ref, gk_ref, gv_ref, gw_ref,
    q_ref, k_ref, v_ref, w_ref, c_ref, spread_ref, gather_ref, rows_ref, pad_ref, unpad_ref,
    wz_rows, wz_send, wz_recv, wg, cot_p, cot_t, go,
    cs0, cs1, cs2, cs3, cs4, cs5, cs6, cr0, cr1, cr2, cr3, cr4, cr5, cr6,
    qc, kc, vc, dc, probs_ref, half_ref, ds_ref, att_a, dq_a, dk_a, dv_a,
    rs, rr, rs_do, rr_do, rt_s, rt_r, racc_k, racc_v, att_ref,
    g1_s, g1_r, g_own, g2_s, g2_r, g3_s, g3_r, g3_own, g4_s, g4_r, g5_s, g5_r,
    isem, ssem, rsem,
):
    cs, cr = (cs0, cs1, cs2, cs3, cs4, cs5, cs6), (cr0, cr1, cr2, cr3, cr4, cr5, cr6)
    dp, ctx = lax.axis_index("dp"), lax.axis_index("ctx")
    core, yh = lax.rem(dp, 2), lax.div(dp, 2)
    x, p = lax.rem(ctx, 4), lax.div(ctx, 4)
    z, yl = lax.rem(p, 16), lax.div(p, 16)
    y = yh * 2 + yl

    loads = [
        pltpu.make_async_copy(src, dst, isem.at[i])
        for i, (src, dst) in enumerate(
            (
                (q_hbm, q_ref), (k_hbm, k_ref), (w_hbm, w_ref), (v_hbm, v_ref), (pad_hbm, pad_ref),
                (c_hbm, c_ref), (spread_hbm, spread_ref), (rows_hbm, rows_ref),
                (gather_hbm, gather_ref), (unpad_hbm, unpad_ref),
            )
        )
    ]
    (load_q, load_k, load_w, load_v, load_pad, load_c, load_spread, load_rows, load_gather,
     load_unpad) = loads
    for load in loads[:3]:
        load.start()

    def at_p(pp):
        return (dp, pp * 4 + x)

    def at_x(xx):
        return (dp, p * 4 + xx)

    def at_y(yy):
        return (lax.div(yy, 2) * 2 + core, lax.rem(yy, 2) * 64 + z * 4 + x)

    def at_core():
        return (yh * 2 + 1 - core, ctx)

    def ring(i, by, n):
        return lax.rem(i + by, n)

    def send(src, dst, sem, where):
        pltpu.make_async_remote_copy(
            src_ref=src, dst_ref=dst, send_sem=ssem.at[sem], recv_sem=rsem.at[sem],
            device_id=where, device_id_type=pl.DeviceIdType.MESH,
        ).start()

    def take(ref, sem):
        pltpu.make_async_copy(ref, ref, rsem.at[sem]).wait()

    def sent(ref, sem):
        pltpu.make_async_copy(ref, ref, ssem.at[sem]).wait()

    barrier = pltpu.get_barrier_semaphore()

    def greet(where):
        pl.semaphore_signal(barrier, inc=1, device_id=where, device_id_type=pl.DeviceIdType.MESH)

    def greet_p(i, _):
        greet(at_p(ring(p, i, GROUP)))
        return 0

    lax.fori_loop(1, GROUP, greet_p, 0)
    for i in range(1, 4):
        greet(at_x(ring(x, i, 4)))
        greet(at_y(ring(y, i, 4)))
    greet(at_core())
    greet(((1 - yh) * 2 + 1 - core, ctx))
    for load in loads[3:]:
        load.start()

    def pack(slot, pairs):
        def one(m, _):
            rows = pl.ds(pl.multiple_of(m * 16, 16), 16)
            for t, ((a_ref, a0), (b_ref, b0)) in enumerate(pairs):
                a = a_ref[rows, a0 : a0 + 128].astype(F32)
                b = b_ref[rows, b0 : b0 + 128].astype(F32)
                lanes = slice(t * 128, (t + 1) * 128)
                cs[slot][2 * m, :, lanes] = jnp.concatenate([a[:8], b[:8]], 0).astype(BF16)
                cs[slot][2 * m + 1, :, lanes] = jnp.concatenate([a[8:], b[8:]], 0).astype(BF16)
            return 0

        lax.fori_loop(0, 16, one, 0)

    def exchange(slot):
        def one(i, _):
            half = lax.div(i + 1, 2)
            odd = lax.rem(i, 2)
            pp = ring(p, odd * half + (1 - odd) * (GROUP - half), GROUP)
            send(cs[slot].at[pp], cr[slot].at[p], slot, at_p(pp))
            return 0

        lax.fori_loop(1, GROUP, one, 0)
        cr[slot][p] = cs[slot][p]

    def unpack(slot, pairs):
        take(cr[slot].at[pl.ds(0, GROUP - 1)], slot)

        def one(m, _):
            rows = pl.ds(pl.multiple_of(m * 16, 16), 16)
            for t, ((a_ref, a0), (b_ref, b0)) in enumerate(pairs):
                lanes = slice(t * 128, (t + 1) * 128)
                first = cr[slot][2 * m, :, lanes].astype(F32)
                second = cr[slot][2 * m + 1, :, lanes].astype(F32)
                a_ref[rows, a0 : a0 + 128] = jnp.concatenate([first[:8], second[:8]], 0).astype(BF16)
                b_ref[rows, b0 : b0 + 128] = jnp.concatenate([first[8:], second[8:]], 0).astype(BF16)
            return 0

        lax.fori_loop(0, 16, one, 0)

    load_q.wait()
    load_k.wait()
    pack(0, [((q_ref, WIDTH + t), (k_ref, WIDTH + t)) for t in (0, 128, 256)])
    load_w.wait()
    w = w_ref[...].astype(F32)
    w = jnp.where(core == 0, w[:, :WIDTH], w[:, WIDTH:])
    w = jnp.where(yh == 0, w[0:3], w[3:6])
    wz_rows[...] = jnp.zeros((16, 128), F32)
    for r in range(3):
        for t in range(3):
            wz_rows[r * 3 + t : r * 3 + t + 1, :] = w[r : r + 1, t * 128 : (t + 1) * 128]
    wz_send[...] = wz_rows[...].astype(BF16)
    wz_recv[z] = wz_send[...]
    pl.semaphore_wait(barrier, 39)

    def send_w(i, _):
        send(wz_send, wz_recv.at[z], WZ, at_p(yl * 16 + ring(z, i, NZ)))
        return 0

    lax.fori_loop(1, NZ, send_w, 0)
    exchange(0)

    load_pad.wait()
    load_v.wait()
    for index, ref in enumerate((q_ref, k_ref, v_ref)):
        padded = dot(ref[:, :WIDTH], pad_ref[...]).astype(BF16)
        for h in range(HEADS):
            rs[h, index] = padded[:, h * 128 : (h + 1) * 128]
    for i in range(1, 4):
        xx = ring(x, i, 4)
        send(rs.at[xx], rr.at[x], RQ, at_x(xx))
    rr[x] = rs[x]

    load_rows.wait()
    take(wz_recv.at[pl.ds(0, NZ - 1)], WZ)
    gathered = wz_recv[...].reshape(256, 128)
    at = yl * 4 + x
    for t in range(3):
        wg[core, yh, at, :, t * 128 : (t + 1) * 128] = dot(rows_ref[t], gathered).astype(BF16)
    own = wg.at[core, yh, at]
    for i in range(1, 4):
        send(own, own, WX, at_x(ring(x, i, 4)))

    load_c.wait()
    load_spread.wait()
    cot_p[...] = dot(c_ref[...], spread_ref[...]).astype(BF16)

    mine = wg.at[core, yh, pl.ds(yl * 4, 4)]
    take(wg.at[core, yh, pl.ds(0, 3)], WX)
    for i in (1, 3, 2):
        send(mine, mine, WY + i - 1, at_y(ring(y, i, 4)))
    send(mine, mine, WC, at_core())
    load_gather.wait()
    cot_t[...] = dot(gather_ref[...], c_ref[...], NT).astype(BF16)
    for i in (1, 3, 2):
        yy = ring(y, 4 - i, 4)
        part = wg.at[core, lax.div(yy, 2), pl.ds(lax.rem(yy, 2) * 4, 4)]
        take(part, WY + i - 1)
        send(part, part, WC + i, at_core())
    for i in range(4):
        take(mine, WC + i)

    def grad_out(c):
        go[:, c * WIDTH : (c + 1) * WIDTH] = dot(
            cot_p[...], wg[c].reshape(768, WIDTH)
        ).astype(BF16)

    grad_out(1)
    pack(1, [((v_ref, WIDTH + t), (go, WIDTH + t)) for t in (0, 128)])
    exchange(1)
    pack(2, [((v_ref, WIDTH + 256), (go, WIDTH + 256))])
    exchange(2)
    grad_out(0)
    padded = dot(go[:, :WIDTH], pad_ref[...]).astype(BF16)
    for h in range(HEADS):
        rs_do[h] = padded[:, h * 128 : (h + 1) * 128]
    for i in range(1, 4):
        xx = ring(x, i, 4)
        send(rs_do.at[xx], rr_do.at[x], RD, at_x(xx))
    rr_do[x] = rs_do[x]

    unpack(0, [((qc, t), (kc, t)) for t in (0, 128, 256)])
    row_at = lax.broadcasted_iota(jnp.int32, (ROWS, ROWS), 0)
    key_at = lax.broadcasted_iota(jnp.int32, (ROWS, ROWS), 1)
    lanes = lax.broadcasted_iota(jnp.int32, (ROWS, WIDTH), 1)

    def span(h):
        return h * HS // 128 * 128, -(-(h + 1) * HS // 128) * 128

    def head(ref, h):
        lo, hi = span(h)
        at = lanes[:, lo:hi]
        value = ref[:, lo:hi]
        return jnp.where((at >= h * HS) & (at < (h + 1) * HS), value, jnp.zeros_like(value))

    def put(ref, h, value):
        lo, hi = span(h)
        for t in range(lo, hi, 128):
            if h > 0 and t == lo:
                ref[:, t : t + 128] += value[:, t - lo : t - lo + 128]
            else:
                ref[:, t : t + 128] = value[:, t - lo : t - lo + 128]

    def softmax(scores):
        top = jnp.max(scores, axis=1, keepdims=True)
        total = top + jnp.log(jnp.sum(jnp.exp(scores - top), axis=1, keepdims=True))
        return jnp.exp(scores - total)

    for h in range(HEADS):
        lo, hi = span(h)
        scores = dot(head(qc, h), kc[:, lo:hi], NT) * SCALE
        allowed = (key_at <= row_at) & (lax.rem(row_at - key_at, CLASSES) == 0)
        probs = softmax(jnp.where(allowed, scores, -1e30))
        probs_ref[h] = probs
        half_ref[h] = probs.astype(BF16)

    take(rr.at[pl.ds(0, 3)], RQ)
    take(rr_do.at[pl.ds(0, 3)], RD)
    racc_k[...] = jnp.zeros_like(racc_k)
    racc_v[...] = jnp.zeros_like(racc_v)
    for i in range(4):
        n = (i + 1) * ROWS
        query, out = rr[i, 0], rr_do[i]
        keys = rr[0 : i + 1, 1].reshape(n, 128)
        values = rr[0 : i + 1, 2].reshape(n, 128)
        at = lax.broadcasted_iota(jnp.int32, (ROWS, n), 0) + i * ROWS
        allowed = lax.broadcasted_iota(jnp.int32, (ROWS, n), 1) <= at
        probs = softmax(jnp.where(allowed, dot(query, keys, NT) * SCALE, -1e30))
        half = probs.astype(BF16)
        attended = dot(half, values).astype(BF16)
        deltas = jnp.sum(out.astype(F32) * attended.astype(F32), axis=1, keepdims=True)
        dscores = (probs * (dot(out, values, NT) - deltas) * SCALE).astype(BF16)
        rt_s[i, 0] = attended
        rt_s[i, 1] = dot(dscores, keys).astype(BF16)
        racc_k[0:n, :] += dot(dscores, query, TN)
        racc_v[0:n, :] += dot(half, out, TN)
    for i in range(4):
        rt_s[i, 2] = racc_k[i * ROWS : (i + 1) * ROWS, :].astype(BF16)
        rt_s[i, 3] = racc_v[i * ROWS : (i + 1) * ROWS, :].astype(BF16)
    for i in range(1, 4):
        xx = ring(x, i, 4)
        send(rt_s.at[xx], rt_r.at[x], RT, at_x(xx))
    rt_r[x] = rt_s[x]

    def attend(h):
        put(att_a, h, dot(half_ref[h], head(vc, h)).astype(BF16).astype(F32))

    def score_grads(h):
        lo, hi = span(h)
        out = head(dc, h)
        deltas = jnp.sum(out.astype(F32) * att_a[:, lo:hi], axis=1, keepdims=True)
        dprobs = dot(out, vc[:, lo:hi], NT)
        dscores = (probs_ref[h] * (dprobs - deltas) * SCALE).astype(BF16)
        ds_ref[h] = dscores
        put(dq_a, h, dot(dscores, head(kc, h)))

    def key_grads(h):
        put(dk_a, h, dot(ds_ref[h], head(qc, h), TN))
        put(dv_a, h, dot(half_ref[h], head(dc, h), TN))

    unpack(1, [((vc, t), (dc, t)) for t in (0, 128)])
    for h in (0, 1):
        attend(h)
        score_grads(h)
    pack(3, [((att_a, 0), (dq_a, 0))])
    exchange(3)
    for h in (0, 1):
        key_grads(h)
    unpack(2, [((vc, 256), (dc, 256))])
    for h in (2, 3):
        attend(h)
    pack(4, [((att_a, 128), (att_a, 256))])
    exchange(4)
    for h in (2, 3):
        score_grads(h)
    pack(5, [((dk_a, 0), (dv_a, 0)), ((dq_a, 128), (dq_a, 256))])
    exchange(5)
    for h in (2, 3):
        key_grads(h)
    pack(6, [((dk_a, 128), (dk_a, 256)), ((dv_a, 128), (dv_a, 256))])
    exchange(6)

    def reduce_core(g):
        attended = att_ref[:, g * WIDTH : (g + 1) * WIDTH]
        theirs = pl.ds(pl.multiple_of((1 - core) * 512, 512), 512)
        ours = pl.ds(pl.multiple_of(core * 512, 512), 512)
        g1_s[g] = dot(cot_t[theirs, :], attended).astype(BF16)
        send(g1_s.at[g], g1_r.at[g], G1 + g, at_core())
        g_own[g] = dot(cot_t[ours, :], attended).reshape(4, 128, WIDTH)

    def reduce_x(g):
        take(g1_r.at[g], G1 + g)
        total = g_own[g] + g1_r[g].astype(F32).reshape(4, 128, WIDTH)
        g_own[g] = total
        g2_s[g] = total.astype(BF16)
        for i in (1, 3, 2):
            xx = ring(x, i, 4)
            send(g2_s.at[g, xx], g2_r.at[g, i - 1], G2 + g, at_x(xx))

    def reduce_y(g):
        take(g2_r.at[g], G2 + g)
        total = g_own[g, x]
        for i in range(3):
            total = total + g2_r[g, i].astype(F32)
        g3_own[g] = total.reshape(4, 32, WIDTH)
        g3_s[g] = total.reshape(4, 32, WIDTH).astype(BF16)
        for i in (1, 3, 2):
            yy = ring(y, i, 4)
            send(g3_s.at[g, lax.rem(yy, 2) * 2 + lax.div(yy, 2)], g3_r.at[g, i - 1], G3 + g, at_y(yy))

    def reduce_z(g):
        take(g3_r.at[g], G3 + g)
        total = g3_own[g, yl * 2 + yh]
        for i in range(3):
            total = total + g3_r[g, i].astype(F32)
        g4_s[g] = total.reshape(4, 8, WIDTH)
        for i in range(4):
            zz = core * 8 + yh * 4 + i

            @pl.when(zz != z)
            def _():
                send(g4_s.at[g, i], g4_r.at[g, z], G4 + g, at_p(yl * 16 + zz))

    owner = (lax.div(z, 8) == core) & (lax.rem(lax.div(z, 4), 2) == yh)

    def reduce_last(g):
        @pl.when(owner)
        def _():
            take(g4_r.at[g, pl.ds(0, NZ - 1)], G4 + g)
            g4_r[g, z] = g4_s[g, lax.rem(z, 4)]
            g5_s[g] = jnp.sum(g4_r[g], axis=0)
            for c in (1, 2, 3):
                send(g5_s.at[g], g5_r.at[g], G5 + g, (ring(dp, c, 4), ctx))

    def finish(g):
        @pl.when(owner)
        def _():
            gw_ref[:, g * WIDTH : (g + 1) * WIDTH] = g5_s[g, 0:6, :]

        @pl.when(jnp.logical_not(owner))
        def _():
            take(g5_r.at[g], G5 + g)
            gw_ref[:, g * WIDTH : (g + 1) * WIDTH] = g5_r[g, 0:6, :]

    load_unpad.wait()
    take(rt_r.at[pl.ds(0, 3)], RT)
    for index, ref in enumerate((att_ref, gq_ref, gk_ref, gv_ref)):
        heads = jnp.concatenate([rt_r[h, index] for h in range(HEADS)], axis=1)
        ref[:, :WIDTH] = dot(heads, unpad_ref[...]).astype(BF16)
    reduce_core(0)
    reduce_x(0)
    unpack(3, [((att_ref, WIDTH), (gq_ref, WIDTH))])
    reduce_y(0)
    unpack(4, [((att_ref, WIDTH + 128), (att_ref, WIDTH + 256))])
    reduce_core(1)
    reduce_z(0)
    reduce_x(1)
    reduce_y(1)
    reduce_last(0)
    reduce_z(1)
    finish(0)
    unpack(5, [((gk_ref, WIDTH), (gv_ref, WIDTH)), ((gq_ref, WIDTH + 128), (gq_ref, WIDTH + 256))])
    reduce_last(1)
    finish(1)
    unpack(6, [((gk_ref, WIDTH + 128), (gk_ref, WIDTH + 256)), ((gv_ref, WIDTH + 128), (gv_ref, WIDTH + 256))])

    for slot in range(7):
        sent(cs[slot].at[pl.ds(0, GROUP - 1)], slot)
    sent(wz_recv.at[pl.ds(0, NZ - 1)], WZ)
    sent(rs.at[pl.ds(0, 3)], RQ)
    sent(wg.at[core, yh, pl.ds(0, 3)], WX)
    for i in range(3):
        sent(mine, WY + i)
    for i in range(4):
        sent(mine, WC + i)
    sent(rs_do.at[pl.ds(0, 3)], RD)
    sent(rt_s.at[pl.ds(0, 3)], RT)
    for g in range(2):
        sent(g1_s.at[g], G1 + g)
        sent(g2_s.at[g, pl.ds(0, 3)], G2 + g)
        sent(g3_s.at[g, pl.ds(0, 3)], G3 + g)

        @pl.when(owner)
        def _():
            sent(g4_s.at[g, pl.ds(0, 3)], G4 + g)
            sent(g4_s.at[g, pl.ds(0, 3)], G5 + g)

        @pl.when(jnp.logical_not(owner))
        def _():
            sent(g4_s.at[g], G4 + g)


def hand_over(*refs):
    half = len(refs) // 2
    for src, dst in zip(refs[:half], refs[half:], strict=True):
        dst[...] = src[...].reshape(dst.shape)


def body(queries, key_rows, value_rows, out_weight, cotangent, *matrices):
    vmem, hbm = pl.BlockSpec(memory_space=pltpu.VMEM), pl.BlockSpec(memory_space=pl.ANY)
    tokens = jax.ShapeDtypeStruct((ROWS, 2 * WIDTH), BF16)
    weight = jax.ShapeDtypeStruct((6, 2 * WIDTH), F32)
    inputs = (queries[0], key_rows[0], value_rows[0], out_weight, cotangent[0], *matrices)
    messages = [pltpu.VMEM((GROUP, 16, 128 * t), BF16) for t in TILES]
    outs = pl.pallas_call(
        kernel,
        out_shape=(tokens, tokens, tokens, weight),
        in_specs=[hbm] * len(inputs),
        out_specs=(vmem,) * 4,
        scratch_shapes=[pltpu.VMEM(a.shape, a.dtype) for a in inputs]
        + [
            pltpu.VMEM((16, 128), F32),
            pltpu.VMEM((16, 128), BF16),
            pltpu.VMEM((NZ, 16, 128), BF16),
            pltpu.VMEM((2, 2, 8, 48, WIDTH), BF16),
            pltpu.VMEM((ROWS, 768), BF16),
            pltpu.VMEM((1024, ROWS), BF16),
            pltpu.VMEM((ROWS, 2 * WIDTH), BF16),
            *messages,
            *messages,
            pltpu.VMEM((ROWS, WIDTH), BF16),
            pltpu.VMEM((ROWS, WIDTH), BF16),
            pltpu.VMEM((ROWS, WIDTH), BF16),
            pltpu.VMEM((ROWS, WIDTH), BF16),
            pltpu.VMEM((HEADS, ROWS, ROWS), F32),
            pltpu.VMEM((HEADS, ROWS, ROWS), BF16),
            pltpu.VMEM((HEADS, ROWS, ROWS), BF16),
            pltpu.VMEM((ROWS, WIDTH), F32),
            pltpu.VMEM((ROWS, WIDTH), F32),
            pltpu.VMEM((ROWS, WIDTH), F32),
            pltpu.VMEM((ROWS, WIDTH), F32),
            pltpu.VMEM((4, 3, ROWS, 128), BF16),
            pltpu.VMEM((4, 3, ROWS, 128), BF16),
            pltpu.VMEM((4, ROWS, 128), BF16),
            pltpu.VMEM((4, ROWS, 128), BF16),
            pltpu.VMEM((4, 4, ROWS, 128), BF16),
            pltpu.VMEM((4, 4, ROWS, 128), BF16),
            pltpu.VMEM((1024, 128), F32),
            pltpu.VMEM((1024, 128), F32),
            pltpu.VMEM((ROWS, 2 * WIDTH), BF16),
            pltpu.VMEM((2, 512, WIDTH), BF16),
            pltpu.VMEM((2, 512, WIDTH), BF16),
            pltpu.VMEM((2, 4, 128, WIDTH), F32),
            pltpu.VMEM((2, 4, 128, WIDTH), BF16),
            pltpu.VMEM((2, 3, 128, WIDTH), BF16),
            pltpu.VMEM((2, 4, 32, WIDTH), BF16),
            pltpu.VMEM((2, 3, 32, WIDTH), BF16),
            pltpu.VMEM((2, 4, 32, WIDTH), F32),
            pltpu.VMEM((2, 4, 8, WIDTH), F32),
            pltpu.VMEM((2, NZ, 8, WIDTH), F32),
            pltpu.VMEM((2, 8, WIDTH), F32),
            pltpu.VMEM((2, 8, WIDTH), F32),
            pltpu.SemaphoreType.DMA((len(inputs),)),
            pltpu.SemaphoreType.DMA((SEMS,)),
            pltpu.SemaphoreType.DMA((SEMS,)),
        ],
        compiler_params=pltpu.CompilerParams(
            collective_id=0, has_side_effects=True, vmem_limit_bytes=48 * 1024 * 1024
        ),
        cost_estimate=pl.CostEstimate(
            flops=8_000_000_000, bytes_accessed=8_000_000, transcendentals=2_000_000
        ),
        name="strided_attention",
    )(*inputs)
    whole = jax.ShapeDtypeStruct((1, ROWS, 2 * WIDTH), BF16)
    return pl.pallas_call(
        hand_over,
        out_shape=(whole, whole, whole, weight),
        in_specs=[vmem] * 4,
        out_specs=(vmem,) * 4,
        name="hand_over",
    )(*outs)


def solution(mesh):
    tokens, rows = P("dp", "ctx", None), P("ctx", None)
    matrices = selections()
    mapped = jax.shard_map(
        body,
        mesh=mesh,
        in_specs=(tokens, tokens, tokens, rows, tokens) + (P(None, None),) * len(matrices),
        out_specs=(tokens, tokens, tokens, rows),
        check_vma=False,
    )

    def run(queries, key_rows, value_rows, out_weight, cotangent):
        return mapped(queries, key_rows, value_rows, out_weight, cotangent, *matrices)

    return run
```

```python
import jax
import jax.numpy as jnp
import numpy as np
from jax import lax
from jax.experimental import pallas as pl
from jax.experimental.pallas import tpu as pltpu
from jax.sharding import PartitionSpec as P

HS = 96
HEADS = 4
WIDTH = HEADS * HS
NX, NZ = 4, 16
GROUP = 32
ROWS = 256
CLASSES = 8
SCALE = HS**-0.5
F32, BF16 = jnp.float32, jnp.bfloat16
NT = (((1,), (1,)), ((), ()))
TN = (((0,), (0,)), ((), ()))


def dot(a, b, dims=None):
    if dims is None:
        return jnp.dot(a, b, preferred_element_type=F32)
    return lax.dot_general(a, b, dims, preferred_element_type=F32)


def selections():
    spread = np.zeros((768, 768), np.float32)
    gather = np.zeros((1024, 768), np.float32)
    for yl in range(2):
        for z in range(NZ):
            for x in range(NX):
                for r in range(6):
                    f = (yl * 64 + z * 4 + x) * 6 + r
                    spread[f, (((r // 3 * 2 + yl) * 4 + x) * 16 + z) * 3 + r % 3] = 1
                    gather[(((z // 8 * 4 + x) * 2 + yl) * 8 + z % 8) * 8 + r, f] = 1
    rows = np.zeros((3, 48, 256), np.float32)
    for t in range(3):
        for z in range(NZ):
            for r in range(3):
                rows[t, z * 3 + r, z * 16 + r * 3 + t] = 1
    pad = np.zeros((WIDTH, 512), np.float32)
    for h in range(HEADS):
        for i in range(HS):
            pad[h * HS + i, h * 128 + i] = 1
    return [jnp.asarray(m, BF16) for m in (spread, gather, rows, pad, pad.T)]


WZ, WX, WY, WC, RQ, RD, RT, G1, G2, G3, G4 = 8, 9, 10, 13, 17, 18, 19, 20, 22, 24, 25
SEMS = 26
TILES = (4, 1, 1, 1, 1, 2, 1, 1)


def kernel(
    q_hbm, k_hbm, v_hbm, w_hbm, c_hbm, spread_hbm, gather_hbm, rows_hbm, pad_hbm, unpad_hbm,
    gq_ref, gk_ref, gv_ref, gw_ref,
    q_ref, k_ref, v_ref, w_ref, c_ref, spread_ref, gather_ref, rows_ref, pad_ref, unpad_ref,
    wz_rows, wz_send, wz_recv, wg, cot_p, cot_t, go,
    cs0, cs1, cs2, cs3, cs4, cs5, cs6, cs7, cr0, cr1, cr2, cr3, cr4, cr5, cr6, cr7,
    qc, kc, vc, dc, probs_ref, half_ref, ds_ref, att_a, dq_a, dk_a, dv_a,
    rs, rr, rs_do, rr_do, rt_s, rt_r, racc_k, racc_v, att_ref,
    g1_s, g1_r, g_own, g2_s, g2_r, g_sum, g3_s, g3_r, g4_s, g4_r,
    isem, ssem, rsem,
):
    cs = (cs0, cs1, cs2, cs3, cs4, cs5, cs6, cs7)
    cr = (cr0, cr1, cr2, cr3, cr4, cr5, cr6, cr7)
    dp, ctx = lax.axis_index("dp"), lax.axis_index("ctx")
    core, yh = lax.rem(dp, 2), lax.div(dp, 2)
    x, p = lax.rem(ctx, 4), lax.div(ctx, 4)
    z, yl = lax.rem(p, 16), lax.div(p, 16)
    y = yh * 2 + yl
    chunk = x * 4 + yl * 2 + yh

    loads = [
        pltpu.make_async_copy(src, dst, isem.at[i])
        for i, (src, dst) in enumerate(
            (
                (q_hbm, q_ref), (k_hbm, k_ref), (v_hbm, v_ref), (w_hbm, w_ref), (pad_hbm, pad_ref),
                (c_hbm, c_ref), (spread_hbm, spread_ref), (rows_hbm, rows_ref),
                (gather_hbm, gather_ref), (unpad_hbm, unpad_ref),
            )
        )
    ]
    (load_q, load_k, load_v, load_w, load_pad, load_c, load_spread, load_rows, load_gather,
     load_unpad) = loads
    for load in loads[:4]:
        load.start()

    def at_p(pp):
        return (dp, pp * 4 + x)

    def at_x(xx):
        return (dp, p * 4 + xx)

    def at_y(yy):
        return (lax.div(yy, 2) * 2 + core, lax.rem(yy, 2) * 64 + z * 4 + x)

    def at_chunk(c):
        return (lax.rem(c, 2) * 2 + core, lax.rem(lax.div(c, 2), 2) * 64 + z * 4 + lax.div(c, 4))

    def at_core():
        return (yh * 2 + 1 - core, ctx)

    def ring(i, by, n):
        return lax.rem(i + by, n)

    def send(src, dst, sem, where):
        pltpu.make_async_remote_copy(
            src_ref=src, dst_ref=dst, send_sem=ssem.at[sem], recv_sem=rsem.at[sem],
            device_id=where, device_id_type=pl.DeviceIdType.MESH,
        ).start()

    def take(ref, sem):
        pltpu.make_async_copy(ref, ref, rsem.at[sem]).wait()

    def sent(ref, sem):
        pltpu.make_async_copy(ref, ref, ssem.at[sem]).wait()

    barrier = pltpu.get_barrier_semaphore()

    def greet(where):
        pl.semaphore_signal(barrier, inc=1, device_id=where, device_id_type=pl.DeviceIdType.MESH)

    def greet_p(i, _):
        greet(at_p(ring(p, i, GROUP)))
        return 0

    lax.fori_loop(1, GROUP, greet_p, 0)


    def greet_chunk(i, _):
        greet(at_chunk(ring(chunk, i, 16)))
        return 0

    lax.fori_loop(1, 16, greet_chunk, 0)
    greet(at_core())
    greet(((1 - yh) * 2 + 1 - core, ctx))
    for load in loads[4:]:
        load.start()

    def pack(slot, pairs):
        def one(m, _):
            rows = pl.ds(pl.multiple_of(m * 16, 16), 16)
            for t, ((a_ref, a0), (b_ref, b0)) in enumerate(pairs):
                a = a_ref[rows, a0 : a0 + 128].astype(F32)
                b = b_ref[rows, b0 : b0 + 128].astype(F32)
                lanes = slice(t * 128, (t + 1) * 128)
                cs[slot][2 * m, :, lanes] = jnp.concatenate([a[:8], b[:8]], 0).astype(BF16)
                cs[slot][2 * m + 1, :, lanes] = jnp.concatenate([a[8:], b[8:]], 0).astype(BF16)
            return 0

        lax.fori_loop(0, 16, one, 0)

    def exchange(slot):
        def one(i, _):
            half = lax.div(i + 1, 2)
            odd = lax.rem(i, 2)
            pp = ring(p, odd * half + (1 - odd) * (GROUP - half), GROUP)
            send(cs[slot].at[pp], cr[slot].at[p], slot, at_p(pp))
            return 0

        lax.fori_loop(1, GROUP, one, 0)
        cr[slot][p] = cs[slot][p]

    def unpack(slot, pairs):
        take(cr[slot].at[pl.ds(0, GROUP - 1)], slot)

        def one(m, _):
            rows = pl.ds(pl.multiple_of(m * 16, 16), 16)
            for t, ((a_ref, a0), (b_ref, b0)) in enumerate(pairs):
                lanes = slice(t * 128, (t + 1) * 128)
                first = cr[slot][2 * m, :, lanes].astype(F32)
                second = cr[slot][2 * m + 1, :, lanes].astype(F32)
                a_ref[rows, a0 : a0 + 128] = jnp.concatenate([first[:8], second[:8]], 0).astype(BF16)
                b_ref[rows, b0 : b0 + 128] = jnp.concatenate([first[8:], second[8:]], 0).astype(BF16)
            return 0

        lax.fori_loop(0, 16, one, 0)

    load_q.wait()
    load_k.wait()
    load_v.wait()
    pack(
        0,
        [((q_ref, WIDTH + t), (k_ref, WIDTH + t)) for t in (0, 128, 256)]
        + [((v_ref, WIDTH), (v_ref, WIDTH + 128))],
    )
    load_w.wait()
    w = w_ref[...].astype(F32)
    w = jnp.where(core == 0, w[:, :WIDTH], w[:, WIDTH:])
    w = jnp.where(yh == 0, w[0:3], w[3:6])
    wz_rows[...] = jnp.zeros((16, 128), F32)
    for r in range(3):
        for t in range(3):
            wz_rows[r * 3 + t : r * 3 + t + 1, :] = w[r : r + 1, t * 128 : (t + 1) * 128]
    wz_send[...] = wz_rows[...].astype(BF16)
    wz_recv[z] = wz_send[...]
    pl.semaphore_wait(barrier, 48)

    def send_w(i, _):
        send(wz_send, wz_recv.at[z], WZ, at_p(yl * 16 + ring(z, i, NZ)))
        return 0

    lax.fori_loop(1, NZ, send_w, 0)
    exchange(0)

    load_pad.wait()
    for index, ref in enumerate((q_ref, k_ref, v_ref)):
        padded = dot(ref[:, :WIDTH], pad_ref[...]).astype(BF16)
        for h in range(HEADS):
            rs[h, index] = padded[:, h * 128 : (h + 1) * 128]
    for i in range(1, 4):
        xx = ring(x, i, 4)
        send(rs.at[xx], rr.at[x], RQ, at_x(xx))
    rr[x] = rs[x]

    load_rows.wait()
    take(wz_recv.at[pl.ds(0, NZ - 1)], WZ)
    at = yl * 4 + x
    gathered = wz_recv[...].reshape(256, 128)
    for t in range(3):
        wg[core, yh, at, :, t * 128 : (t + 1) * 128] = dot(rows_ref[t], gathered).astype(BF16)
    own = wg.at[core, yh, at]
    for i in range(1, 4):
        send(own, own, WX, at_x(ring(x, i, 4)))

    load_c.wait()
    load_spread.wait()
    cot_p[...] = dot(c_ref[...], spread_ref[...]).astype(BF16)

    mine = wg.at[core, yh, pl.ds(yl * 4, 4)]
    take(wg.at[core, yh, pl.ds(0, 3)], WX)
    for i in (1, 3, 2):
        send(mine, mine, WY + i - 1, at_y(ring(y, i, 4)))
    send(mine, mine, WC, at_core())
    load_gather.wait()
    cot_t[...] = dot(gather_ref[...], c_ref[...], NT).astype(BF16)
    for i in (1, 3, 2):
        yy = ring(y, 4 - i, 4)
        part = wg.at[core, lax.div(yy, 2), pl.ds(lax.rem(yy, 2) * 4, 4)]
        take(part, WY + i - 1)
        send(part, part, WC + i, at_core())
    for i in range(4):
        take(mine, WC + i)

    def grad_out(c):
        go[:, c * WIDTH : (c + 1) * WIDTH] = dot(
            cot_p[...], wg[c].reshape(768, WIDTH)
        ).astype(BF16)

    grad_out(1)
    pack(1, [((go, WIDTH), (go, WIDTH + 128))])
    exchange(1)
    pack(2, [((go, WIDTH + 256), (v_ref, WIDTH + 256))])
    exchange(2)
    grad_out(0)
    padded = dot(go[:, :WIDTH], pad_ref[...]).astype(BF16)
    for h in range(HEADS):
        rs_do[h] = padded[:, h * 128 : (h + 1) * 128]
    for i in range(1, 4):
        xx = ring(x, i, 4)
        send(rs_do.at[xx], rr_do.at[x], RD, at_x(xx))
    rr_do[x] = rs_do[x]

    unpack(0, [((qc, t), (kc, t)) for t in (0, 128, 256)] + [((vc, 0), (vc, 128))])
    row_at = lax.broadcasted_iota(jnp.int32, (ROWS, ROWS), 0)
    key_at = lax.broadcasted_iota(jnp.int32, (ROWS, ROWS), 1)
    lanes = lax.broadcasted_iota(jnp.int32, (ROWS, WIDTH), 1)

    def span(h):
        return h * HS // 128 * 128, -(-(h + 1) * HS // 128) * 128

    def head(ref, h):
        lo, hi = span(h)
        at = lanes[:, lo:hi]
        value = ref[:, lo:hi]
        return jnp.where((at >= h * HS) & (at < (h + 1) * HS), value, jnp.zeros_like(value))

    def put(ref, h, value):
        lo, hi = span(h)
        for t in range(lo, hi, 128):
            if h > 0 and t == lo:
                ref[:, t : t + 128] += value[:, t - lo : t - lo + 128]
            else:
                ref[:, t : t + 128] = value[:, t - lo : t - lo + 128]

    def softmax(scores):
        top = jnp.max(scores, axis=1, keepdims=True)
        total = top + jnp.log(jnp.sum(jnp.exp(scores - top), axis=1, keepdims=True))
        return jnp.exp(scores - total)

    for h in range(HEADS):
        lo, hi = span(h)
        scores = dot(head(qc, h), kc[:, lo:hi], NT) * SCALE
        allowed = (key_at <= row_at) & (lax.rem(row_at - key_at, CLASSES) == 0)
        probs = softmax(jnp.where(allowed, scores, -1e30))
        probs_ref[h] = probs
        half_ref[h] = probs.astype(BF16)

    take(rr.at[pl.ds(0, 3)], RQ)
    take(rr_do.at[pl.ds(0, 3)], RD)
    racc_k[...] = jnp.zeros_like(racc_k)
    racc_v[...] = jnp.zeros_like(racc_v)
    for i in range(4):
        n = (i + 1) * ROWS
        query, out = rr[i, 0], rr_do[i]
        keys = rr[0 : i + 1, 1].reshape(n, 128)
        values = rr[0 : i + 1, 2].reshape(n, 128)
        at = lax.broadcasted_iota(jnp.int32, (ROWS, n), 0) + i * ROWS
        allowed = lax.broadcasted_iota(jnp.int32, (ROWS, n), 1) <= at
        probs = softmax(jnp.where(allowed, dot(query, keys, NT) * SCALE, -1e30))
        half = probs.astype(BF16)
        attended = dot(half, values).astype(BF16)
        deltas = jnp.sum(out.astype(F32) * attended.astype(F32), axis=1, keepdims=True)
        dscores = (probs * (dot(out, values, NT) - deltas) * SCALE).astype(BF16)
        rt_s[i, 0] = attended
        rt_s[i, 1] = dot(dscores, keys).astype(BF16)
        racc_k[0:n, :] += dot(dscores, query, TN)
        racc_v[0:n, :] += dot(half, out, TN)
    for i in range(4):
        rt_s[i, 2] = racc_k[i * ROWS : (i + 1) * ROWS, :].astype(BF16)
        rt_s[i, 3] = racc_v[i * ROWS : (i + 1) * ROWS, :].astype(BF16)
    for i in range(1, 4):
        xx = ring(x, i, 4)
        send(rt_s.at[xx], rt_r.at[x], RT, at_x(xx))
    rt_r[x] = rt_s[x]

    def attend(h):
        put(att_a, h, dot(half_ref[h], head(vc, h)).astype(BF16).astype(F32))

    def score_grads(h):
        lo, hi = span(h)
        out = head(dc, h)
        deltas = jnp.sum(out.astype(F32) * att_a[:, lo:hi], axis=1, keepdims=True)
        dprobs = dot(out, vc[:, lo:hi], NT)
        dscores = (probs_ref[h] * (dprobs - deltas) * SCALE).astype(BF16)
        ds_ref[h] = dscores
        put(dq_a, h, dot(dscores, head(kc, h)))

    def key_grads(h):
        put(dk_a, h, dot(ds_ref[h], head(qc, h), TN))
        put(dv_a, h, dot(half_ref[h], head(dc, h), TN))

    unpack(1, [((dc, 0), (dc, 128))])
    for h in (0, 1):
        attend(h)
        score_grads(h)
    pack(3, [((att_a, 0), (dq_a, 0))])
    exchange(3)
    for h in (0, 1):
        key_grads(h)
    unpack(2, [((dc, 256), (vc, 256))])
    for h in (2, 3):
        attend(h)
    pack(4, [((att_a, 128), (att_a, 256))])
    exchange(4)
    for h in (2, 3):
        score_grads(h)
    pack(5, [((dk_a, 0), (dv_a, 0)), ((dq_a, 128), (dq_a, 256))])
    exchange(5)
    for h in (2, 3):
        key_grads(h)
    pack(6, [((dk_a, 128), (dk_a, 256))])
    exchange(6)
    pack(7, [((dv_a, 128), (dv_a, 256))])

    def reduce_core(g):
        attended = att_ref[:, g * WIDTH : (g + 1) * WIDTH]
        theirs = pl.ds(pl.multiple_of((1 - core) * 512, 512), 512)
        ours = pl.ds(pl.multiple_of(core * 512, 512), 512)
        g1_s[g] = dot(cot_t[theirs, :], attended).astype(BF16)
        send(g1_s.at[g], g1_r.at[g], G1 + g, at_core())
        g_own[g] = dot(cot_t[ours, :], attended).reshape(16, 32, WIDTH)

    def reduce_plane(g):
        take(g1_r.at[g], G1 + g)
        total = g_own[g] + g1_r[g].astype(F32).reshape(16, 32, WIDTH)
        g_own[g] = total
        g2_s[g] = total.astype(BF16)

        def one(i, _):
            c = ring(chunk, i, 16)
            send(g2_s.at[g, c], g2_r.at[g, chunk], G2 + g, at_chunk(c))
            return 0

        lax.fori_loop(1, 16, one, 0)
        g2_r[g, chunk] = jnp.zeros((32, WIDTH), BF16)

    def reduce_z():
        for g in range(2):
            take(g2_r.at[g, pl.ds(0, 15)], G2 + g)
            total = g_own[g, chunk]
            for c in range(16):
                total = total + g2_r[g, c].astype(F32)
            g_sum[g] = total.reshape(4, 8, WIDTH)
        for i in range(4):
            zz = core * 8 + yh * 4 + i
            g3_s[i] = jnp.concatenate([g_sum[0, i], g_sum[1, i]], 0).astype(BF16)

            @pl.when(zz != z)
            def _():
                send(g3_s.at[i], g3_r.at[z], G3, at_p(yl * 16 + zz))

    owner = (lax.div(z, 8) == core) & (lax.rem(lax.div(z, 4), 2) == yh)

    def reduce_last():
        @pl.when(owner)
        def _():
            take(g3_r.at[pl.ds(0, NZ - 1)], G3)
            g3_r[z] = g3_s[lax.rem(z, 4)]
            total = g3_r[0].astype(F32)
            for i in range(1, NZ):
                total = total + g3_r[i].astype(F32)
            g4_s[...] = total
            for c in (1, 2, 3):
                send(g4_s, g4_r, G4, (ring(dp, c, 4), ctx))

    def finish():
        @pl.when(owner)
        def _():
            g4_r[...] = g4_s[...]

        @pl.when(jnp.logical_not(owner))
        def _():
            take(g4_r, G4)

        gw_ref[:, :WIDTH] = g4_r[0:6, :]
        gw_ref[:, WIDTH:] = g4_r[8:14, :]

    load_unpad.wait()
    take(rt_r.at[pl.ds(0, 3)], RT)
    for index, ref in enumerate((att_ref, gq_ref, gk_ref, gv_ref)):
        heads = jnp.concatenate([rt_r[h, index] for h in range(HEADS)], axis=1)
        ref[:, :WIDTH] = dot(heads, unpad_ref[...]).astype(BF16)
    reduce_core(0)
    unpack(3, [((att_ref, WIDTH), (gq_ref, WIDTH))])
    unpack(4, [((att_ref, WIDTH + 128), (att_ref, WIDTH + 256))])
    reduce_core(1)
    reduce_plane(0)
    reduce_plane(1)
    reduce_z()
    exchange(7)
    unpack(5, [((gk_ref, WIDTH), (gv_ref, WIDTH)), ((gq_ref, WIDTH + 128), (gq_ref, WIDTH + 256))])
    reduce_last()
    unpack(6, [((gk_ref, WIDTH + 128), (gk_ref, WIDTH + 256))])
    finish()
    unpack(7, [((gv_ref, WIDTH + 128), (gv_ref, WIDTH + 256))])

    for slot in range(8):
        sent(cs[slot].at[pl.ds(0, GROUP - 1)], slot)
    sent(wz_recv.at[pl.ds(0, NZ - 1)], WZ)
    sent(rs.at[pl.ds(0, 3)], RQ)
    sent(wg.at[core, yh, pl.ds(0, 3)], WX)
    for i in range(3):
        sent(mine, WY + i)
    for i in range(4):
        sent(mine, WC + i)
    sent(rs_do.at[pl.ds(0, 3)], RD)
    sent(rt_s.at[pl.ds(0, 3)], RT)
    for g in range(2):
        sent(g1_s.at[g], G1 + g)
        sent(g2_s.at[g, pl.ds(0, 15)], G2 + g)

    @pl.when(owner)
    def _():
        sent(g3_s.at[pl.ds(0, 3)], G3)
        sent(g_sum.at[pl.ds(0, 2), pl.ds(0, 3)], G4)

    @pl.when(jnp.logical_not(owner))
    def _():
        sent(g3_s, G3)


def hand_over(*refs):
    n = 4
    srcs, dsts, held, sems = refs[:n], refs[n : 2 * n], refs[2 * n : 3 * n], refs[3 * n]
    inward = [pltpu.make_async_copy(a, b, sems.at[0, i]) for i, (a, b) in enumerate(zip(srcs, held, strict=True))]
    outward = [pltpu.make_async_copy(a, b, sems.at[1, i]) for i, (a, b) in enumerate(zip(held, dsts, strict=True))]
    for copy in inward:
        copy.start()
    for first, second in zip(inward, outward, strict=True):
        first.wait()
        second.start()
    for copy in outward:
        copy.wait()


def body(queries, key_rows, value_rows, out_weight, cotangent, *matrices):
    vmem, hbm = pl.BlockSpec(memory_space=pltpu.VMEM), pl.BlockSpec(memory_space=pltpu.HBM)
    tokens = jax.ShapeDtypeStruct((ROWS, 2 * WIDTH), BF16)
    weight = jax.ShapeDtypeStruct((6, 2 * WIDTH), F32)
    inputs = (queries[0], key_rows[0], value_rows[0], out_weight, cotangent[0], *matrices)
    messages = [pltpu.VMEM((GROUP, 16, 128 * t), BF16) for t in TILES]
    outs = pl.pallas_call(
        kernel,
        out_shape=(tokens, tokens, tokens, weight),
        in_specs=[hbm] * len(inputs),
        out_specs=(vmem,) * 4,
        scratch_shapes=[pltpu.VMEM(a.shape, a.dtype) for a in inputs]
        + [
            pltpu.VMEM((16, 128), F32),
            pltpu.VMEM((16, 128), BF16),
            pltpu.VMEM((NZ, 16, 128), BF16),
            pltpu.VMEM((2, 2, 8, 48, WIDTH), BF16),
            pltpu.VMEM((ROWS, 768), BF16),
            pltpu.VMEM((1024, ROWS), BF16),
            pltpu.VMEM((ROWS, 2 * WIDTH), BF16),
            *messages,
            *messages,
            pltpu.VMEM((ROWS, WIDTH), BF16),
            pltpu.VMEM((ROWS, WIDTH), BF16),
            pltpu.VMEM((ROWS, WIDTH), BF16),
            pltpu.VMEM((ROWS, WIDTH), BF16),
            pltpu.VMEM((HEADS, ROWS, ROWS), F32),
            pltpu.VMEM((HEADS, ROWS, ROWS), BF16),
            pltpu.VMEM((HEADS, ROWS, ROWS), BF16),
            pltpu.VMEM((ROWS, WIDTH), F32),
            pltpu.VMEM((ROWS, WIDTH), F32),
            pltpu.VMEM((ROWS, WIDTH), F32),
            pltpu.VMEM((ROWS, WIDTH), F32),
            pltpu.VMEM((4, 3, ROWS, 128), BF16),
            pltpu.VMEM((4, 3, ROWS, 128), BF16),
            pltpu.VMEM((4, ROWS, 128), BF16),
            pltpu.VMEM((4, ROWS, 128), BF16),
            pltpu.VMEM((4, 4, ROWS, 128), BF16),
            pltpu.VMEM((4, 4, ROWS, 128), BF16),
            pltpu.VMEM((1024, 128), F32),
            pltpu.VMEM((1024, 128), F32),
            pltpu.VMEM((ROWS, 2 * WIDTH), BF16),
            pltpu.VMEM((2, 512, WIDTH), BF16),
            pltpu.VMEM((2, 512, WIDTH), BF16),
            pltpu.VMEM((2, 16, 32, WIDTH), F32),
            pltpu.VMEM((2, 16, 32, WIDTH), BF16),
            pltpu.VMEM((2, 16, 32, WIDTH), BF16),
            pltpu.VMEM((2, 4, 8, WIDTH), F32),
            pltpu.VMEM((4, 16, WIDTH), BF16),
            pltpu.VMEM((NZ, 16, WIDTH), BF16),
            pltpu.VMEM((16, WIDTH), F32),
            pltpu.VMEM((16, WIDTH), F32),
            pltpu.SemaphoreType.DMA((len(inputs),)),
            pltpu.SemaphoreType.DMA((SEMS,)),
            pltpu.SemaphoreType.DMA((SEMS,)),
        ],
        compiler_params=pltpu.CompilerParams(
            collective_id=0, has_side_effects=True, vmem_limit_bytes=60 * 1024 * 1024
        ),
        cost_estimate=pl.CostEstimate(
            flops=8_000_000_000, bytes_accessed=8_000_000, transcendentals=2_000_000
        ),
        name="strided_attention",
    )(*inputs)
    outs = pl.pallas_call(
        hand_over,
        out_shape=(tokens, tokens, tokens, weight),
        in_specs=[hbm] * 4,
        out_specs=(hbm,) * 4,
        scratch_shapes=[pltpu.VMEM(a.shape, a.dtype) for a in outs] + [pltpu.SemaphoreType.DMA((2, 4))],
        name="hand_over",
    )(*outs)
    return (outs[0][None], outs[1][None], outs[2][None], outs[3])


def solution(mesh):
    tokens, rows = P("dp", "ctx", None), P("ctx", None)
    matrices = selections()
    mapped = jax.shard_map(
        body,
        mesh=mesh,
        in_specs=(tokens, tokens, tokens, rows, tokens) + (P(None, None),) * len(matrices),
        out_specs=(tokens, tokens, tokens, rows),
        check_vma=False,
    )

    def run(queries, key_rows, value_rows, out_weight, cotangent):
        return mapped(queries, key_rows, value_rows, out_weight, cotangent, *matrices)

    return run
```

```python
import jax
import jax.numpy as jnp
import numpy as np
from jax import lax
from jax.experimental import pallas as pl
from jax.experimental.pallas import tpu as pltpu
from jax.sharding import PartitionSpec as P

HS = 96
HEADS = 4
WIDTH = HEADS * HS
NX, NZ = 4, 16
GROUP = 32
ROWS = 256
CLASSES = 8
SCALE = HS**-0.5
F32, BF16 = jnp.float32, jnp.bfloat16
NT = (((1,), (1,)), ((), ()))
TN = (((0,), (0,)), ((), ()))


def dot(a, b, dims=None):
    if dims is None:
        return jnp.dot(a, b, preferred_element_type=F32)
    return lax.dot_general(a, b, dims, preferred_element_type=F32)


def selections():
    spread = np.zeros((768, 768), np.float32)
    gather = np.zeros((1024, 768), np.float32)
    for yl in range(2):
        for z in range(NZ):
            for x in range(NX):
                for r in range(6):
                    f = (yl * 64 + z * 4 + x) * 6 + r
                    spread[f, (((r // 3 * 2 + yl) * 4 + x) * 16 + z) * 3 + r % 3] = 1
                    gather[(((z // 8 * 4 + x) * 2 + yl) * 8 + z % 8) * 8 + r, f] = 1
    rows = np.zeros((3, 48, 256), np.float32)
    for t in range(3):
        for z in range(NZ):
            for r in range(3):
                rows[t, z * 3 + r, z * 16 + r * 3 + t] = 1
    pad = np.zeros((WIDTH, 512), np.float32)
    for h in range(HEADS):
        for i in range(HS):
            pad[h * HS + i, h * 128 + i] = 1
    return [jnp.asarray(m, BF16) for m in (spread, gather, rows, pad, pad.T)]


WZ, WX, WC, RQ, RD, RT, G1, G2, G3, G4 = 8, 9, 10, 11, 12, 13, 14, 16, 18, 19
SEMS = 20
TILES = (4, 1, 1, 1, 1, 2, 1, 1)


def kernel(
    q_hbm, k_hbm, v_hbm, w_hbm, c_hbm, spread_hbm, gather_hbm, rows_hbm, pad_hbm, unpad_hbm,
    gq_ref, gk_ref, gv_ref, gw_ref,
    q_ref, k_ref, v_ref, w_ref, c_ref, spread_ref, gather_ref, rows_ref, pad_ref, unpad_ref,
    wz_rows, wz_send, wz_recv, wg, cot_p, cot_t, go,
    cs0, cs1, cs2, cs3, cs4, cs5, cs6, cs7, cr0, cr1, cr2, cr3, cr4, cr5, cr6, cr7,
    qc, kc, vc, dc, probs_ref, half_ref, ds_ref, att_a, dq_a, dk_a, dv_a,
    rs, rr, rs_do, rr_do, rt_s, rt_r, racc_k, racc_v, att_ref,
    g1_s, g1_r, g_own, g2_s, g2_r, g_sum, g3_s, g3_r, g4_s, g4_r,
    isem, ssem, rsem, line_sem, plane_sem, core_sem,
):
    cs = (cs0, cs1, cs2, cs3, cs4, cs5, cs6, cs7)
    cr = (cr0, cr1, cr2, cr3, cr4, cr5, cr6, cr7)
    dp, ctx = lax.axis_index("dp"), lax.axis_index("ctx")
    core, yh = lax.rem(dp, 2), lax.div(dp, 2)
    x, p = lax.rem(ctx, 4), lax.div(ctx, 4)
    z, yl = lax.rem(p, 16), lax.div(p, 16)
    y = yh * 2 + yl
    chunk = x * 4 + yl * 2 + yh

    loads = [
        pltpu.make_async_copy(src, dst, isem.at[i])
        for i, (src, dst) in enumerate(
            (
                (q_hbm, q_ref), (k_hbm, k_ref), (v_hbm, v_ref), (w_hbm, w_ref), (pad_hbm, pad_ref),
                (c_hbm, c_ref), (spread_hbm, spread_ref), (rows_hbm, rows_ref),
                (gather_hbm, gather_ref), (unpad_hbm, unpad_ref),
            )
        )
    ]
    (load_q, load_k, load_v, load_w, load_pad, load_c, load_spread, load_rows, load_gather,
     load_unpad) = loads
    for load in loads[:4]:
        load.start()

    def at_p(pp):
        return (dp, pp * 4 + x)

    def at_x(xx):
        return (dp, p * 4 + xx)

    def at_y(yy):
        return (lax.div(yy, 2) * 2 + core, lax.rem(yy, 2) * 64 + z * 4 + x)

    def at_chunk(c):
        return (lax.rem(c, 2) * 2 + core, lax.rem(lax.div(c, 2), 2) * 64 + z * 4 + lax.div(c, 4))

    def at_core():
        return (yh * 2 + 1 - core, ctx)

    def ring(i, by, n):
        return lax.rem(i + by, n)

    def send(src, dst, sem, where):
        pltpu.make_async_remote_copy(
            src_ref=src, dst_ref=dst, send_sem=ssem.at[sem], recv_sem=rsem.at[sem],
            device_id=where, device_id_type=pl.DeviceIdType.MESH,
        ).start()

    def take(ref, sem):
        pltpu.make_async_copy(ref, ref, rsem.at[sem]).wait()

    def sent(ref, sem):
        pltpu.make_async_copy(ref, ref, ssem.at[sem]).wait()

    barrier = pltpu.get_barrier_semaphore()

    def greet(sem, where):
        pl.semaphore_signal(sem, inc=1, device_id=where, device_id_type=pl.DeviceIdType.MESH)

    for i in range(1, NZ):
        greet(barrier, at_p(yl * 16 + ring(z, i, NZ)))
    for i in range(1, 4):
        greet(barrier, at_x(ring(x, i, 4)))
        greet(barrier, at_y(ring(y, i, 4)))
    greet(barrier, at_core())
    for load in loads[4:]:
        load.start()

    def pack(slot, pairs):
        def one(m, _):
            rows = pl.ds(pl.multiple_of(m * 16, 16), 16)
            for t, ((a_ref, a0), (b_ref, b0)) in enumerate(pairs):
                a = a_ref[rows, a0 : a0 + 128].astype(F32)
                b = b_ref[rows, b0 : b0 + 128].astype(F32)
                lanes = slice(t * 128, (t + 1) * 128)
                cs[slot][2 * m, :, lanes] = jnp.concatenate([a[:8], b[:8]], 0).astype(BF16)
                cs[slot][2 * m + 1, :, lanes] = jnp.concatenate([a[8:], b[8:]], 0).astype(BF16)
            return 0

        lax.fori_loop(0, 16, one, 0)

    def exchange(slot):
        def own_line(i, _):
            half = lax.div(i + 1, 2)
            odd = lax.rem(i, 2)
            pp = yl * 16 + ring(z, odd * half + (1 - odd) * (NZ - half), NZ)
            send(cs[slot].at[pp], cr[slot].at[p], slot, at_p(pp))
            return 0

        def other_line(i, _):
            half = lax.div(i + 1, 2)
            odd = lax.rem(i, 2)
            pp = (1 - yl) * 16 + ring(z, odd * half + (1 - odd) * (NZ - half), NZ)
            send(cs[slot].at[pp], cr[slot].at[p], slot, at_p(pp))
            return 0

        lax.fori_loop(1, NZ, own_line, 0)
        if slot == 0:
            pl.semaphore_wait(line_sem, 1)
        lax.fori_loop(0, NZ, other_line, 0)
        cr[slot][p] = cs[slot][p]

    def unpack(slot, pairs):
        take(cr[slot].at[pl.ds(0, GROUP - 1)], slot)

        def one(m, _):
            rows = pl.ds(pl.multiple_of(m * 16, 16), 16)
            for t, ((a_ref, a0), (b_ref, b0)) in enumerate(pairs):
                lanes = slice(t * 128, (t + 1) * 128)
                first = cr[slot][2 * m, :, lanes].astype(F32)
                second = cr[slot][2 * m + 1, :, lanes].astype(F32)
                a_ref[rows, a0 : a0 + 128] = jnp.concatenate([first[:8], second[:8]], 0).astype(BF16)
                b_ref[rows, b0 : b0 + 128] = jnp.concatenate([first[8:], second[8:]], 0).astype(BF16)
            return 0

        lax.fori_loop(0, 16, one, 0)

    load_q.wait()
    load_k.wait()
    load_v.wait()
    pack(
        0,
        [((q_ref, WIDTH + t), (k_ref, WIDTH + t)) for t in (0, 128, 256)]
        + [((v_ref, WIDTH), (v_ref, WIDTH + 128))],
    )
    load_w.wait()
    w = w_ref[...].astype(F32)
    w = jnp.where(core == 0, w[:, :WIDTH], w[:, WIDTH:])
    w = jnp.where(yh == 0, w[0:3], w[3:6])
    wz_rows[...] = jnp.zeros((16, 128), F32)
    for r in range(3):
        for t in range(3):
            wz_rows[r * 3 + t : r * 3 + t + 1, :] = w[r : r + 1, t * 128 : (t + 1) * 128]
    wz_send[...] = wz_rows[...].astype(BF16)
    wz_recv[z] = wz_send[...]
    pl.semaphore_wait(barrier, 22)
    greet(line_sem, at_p((1 - yl) * 16 + z))
    for i in range(1, 4):
        greet(plane_sem, at_x(ring(x, i, 4)))
    greet(core_sem, at_core())

    def send_w(i, _):
        send(wz_send, wz_recv.at[z], WZ, at_p(yl * 16 + ring(z, i, NZ)))
        return 0

    lax.fori_loop(1, NZ, send_w, 0)
    exchange(0)

    load_pad.wait()
    for index, ref in enumerate((q_ref, k_ref, v_ref)):
        padded = dot(ref[:, :WIDTH], pad_ref[...]).astype(BF16)
        for h in range(HEADS):
            rs[h, index] = padded[:, h * 128 : (h + 1) * 128]
    for i in range(1, 4):
        xx = ring(x, i, 4)
        send(rs.at[xx], rr.at[x], RQ, at_x(xx))
    rr[x] = rs[x]

    load_rows.wait()
    take(wz_recv.at[pl.ds(0, NZ - 1)], WZ)
    at = yh * 8 + yl * 4 + x
    gathered = wz_recv[...].reshape(256, 128)
    for t in range(3):
        wg[core, at, :, t * 128 : (t + 1) * 128] = dot(rows_ref[t], gathered).astype(BF16)
    own = wg.at[core, at]
    pl.semaphore_wait(plane_sem, 3)

    def send_plane(i, _):
        send(own, own, WX, at_chunk(ring(chunk, i, 16)))
        return 0

    lax.fori_loop(1, 16, send_plane, 0)

    load_c.wait()
    load_spread.wait()
    cot_p[...] = dot(c_ref[...], spread_ref[...]).astype(BF16)

    load_gather.wait()
    cot_t[...] = dot(gather_ref[...], c_ref[...], NT).astype(BF16)
    take(wg.at[core, pl.ds(0, 15)], WX)
    send(wg.at[core], wg.at[core], WC, at_core())
    take(wg.at[1 - core], WC)

    def grad_out(c):
        go[:, c * WIDTH : (c + 1) * WIDTH] = dot(
            cot_p[...], wg[c].reshape(768, WIDTH)
        ).astype(BF16)

    grad_out(1)
    pack(1, [((go, WIDTH), (go, WIDTH + 128))])
    exchange(1)
    pack(2, [((go, WIDTH + 256), (v_ref, WIDTH + 256))])
    exchange(2)
    grad_out(0)
    padded = dot(go[:, :WIDTH], pad_ref[...]).astype(BF16)
    for h in range(HEADS):
        rs_do[h] = padded[:, h * 128 : (h + 1) * 128]
    for i in range(1, 4):
        xx = ring(x, i, 4)
        send(rs_do.at[xx], rr_do.at[x], RD, at_x(xx))
    rr_do[x] = rs_do[x]

    unpack(0, [((qc, t), (kc, t)) for t in (0, 128, 256)] + [((vc, 0), (vc, 128))])
    row_at = lax.broadcasted_iota(jnp.int32, (ROWS, ROWS), 0)
    key_at = lax.broadcasted_iota(jnp.int32, (ROWS, ROWS), 1)
    lanes = lax.broadcasted_iota(jnp.int32, (ROWS, WIDTH), 1)

    def span(h):
        return h * HS // 128 * 128, -(-(h + 1) * HS // 128) * 128

    def head(ref, h):
        lo, hi = span(h)
        at = lanes[:, lo:hi]
        value = ref[:, lo:hi]
        return jnp.where((at >= h * HS) & (at < (h + 1) * HS), value, jnp.zeros_like(value))

    def put(ref, h, value):
        lo, hi = span(h)
        for t in range(lo, hi, 128):
            if h > 0 and t == lo:
                ref[:, t : t + 128] += value[:, t - lo : t - lo + 128]
            else:
                ref[:, t : t + 128] = value[:, t - lo : t - lo + 128]

    def softmax(scores):
        top = jnp.max(scores, axis=1, keepdims=True)
        total = top + jnp.log(jnp.sum(jnp.exp(scores - top), axis=1, keepdims=True))
        return jnp.exp(scores - total)

    for h in range(HEADS):
        lo, hi = span(h)
        scores = dot(head(qc, h), kc[:, lo:hi], NT) * SCALE
        allowed = (key_at <= row_at) & (lax.rem(row_at - key_at, CLASSES) == 0)
        probs = softmax(jnp.where(allowed, scores, -1e30))
        probs_ref[h] = probs
        half_ref[h] = probs.astype(BF16)

    take(rr.at[pl.ds(0, 3)], RQ)
    take(rr_do.at[pl.ds(0, 3)], RD)
    racc_k[...] = jnp.zeros_like(racc_k)
    racc_v[...] = jnp.zeros_like(racc_v)
    for i in range(4):
        n = (i + 1) * ROWS
        query, out = rr[i, 0], rr_do[i]
        keys = rr[0 : i + 1, 1].reshape(n, 128)
        values = rr[0 : i + 1, 2].reshape(n, 128)
        at = lax.broadcasted_iota(jnp.int32, (ROWS, n), 0) + i * ROWS
        allowed = lax.broadcasted_iota(jnp.int32, (ROWS, n), 1) <= at
        probs = softmax(jnp.where(allowed, dot(query, keys, NT) * SCALE, -1e30))
        half = probs.astype(BF16)
        attended = dot(half, values).astype(BF16)
        deltas = jnp.sum(out.astype(F32) * attended.astype(F32), axis=1, keepdims=True)
        dscores = (probs * (dot(out, values, NT) - deltas) * SCALE).astype(BF16)
        rt_s[i, 0] = attended
        rt_s[i, 1] = dot(dscores, keys).astype(BF16)
        racc_k[0:n, :] += dot(dscores, query, TN)
        racc_v[0:n, :] += dot(half, out, TN)
    for i in range(4):
        rt_s[i, 2] = racc_k[i * ROWS : (i + 1) * ROWS, :].astype(BF16)
        rt_s[i, 3] = racc_v[i * ROWS : (i + 1) * ROWS, :].astype(BF16)
    for i in range(1, 4):
        xx = ring(x, i, 4)
        send(rt_s.at[xx], rt_r.at[x], RT, at_x(xx))
    rt_r[x] = rt_s[x]

    def attend(h):
        put(att_a, h, dot(half_ref[h], head(vc, h)).astype(BF16).astype(F32))

    def score_grads(h):
        lo, hi = span(h)
        out = head(dc, h)
        deltas = jnp.sum(out.astype(F32) * att_a[:, lo:hi], axis=1, keepdims=True)
        dprobs = dot(out, vc[:, lo:hi], NT)
        dscores = (probs_ref[h] * (dprobs - deltas) * SCALE).astype(BF16)
        ds_ref[h] = dscores
        put(dq_a, h, dot(dscores, head(kc, h)))

    def key_grads(h):
        put(dk_a, h, dot(ds_ref[h], head(qc, h), TN))
        put(dv_a, h, dot(half_ref[h], head(dc, h), TN))

    unpack(1, [((dc, 0), (dc, 128))])
    for h in (0, 1):
        attend(h)
        score_grads(h)
    pack(3, [((att_a, 0), (dq_a, 0))])
    exchange(3)
    for h in (0, 1):
        key_grads(h)
    unpack(2, [((dc, 256), (vc, 256))])
    for h in (2, 3):
        attend(h)
    pack(4, [((att_a, 128), (att_a, 256))])
    exchange(4)
    for h in (2, 3):
        score_grads(h)
    pack(5, [((dk_a, 0), (dv_a, 0)), ((dq_a, 128), (dq_a, 256))])
    exchange(5)
    for h in (2, 3):
        key_grads(h)
    pack(6, [((dk_a, 128), (dk_a, 256))])
    exchange(6)
    pack(7, [((dv_a, 128), (dv_a, 256))])

    def reduce_core(g):
        attended = att_ref[:, g * WIDTH : (g + 1) * WIDTH]
        theirs = pl.ds(pl.multiple_of((1 - core) * 512, 512), 512)
        ours = pl.ds(pl.multiple_of(core * 512, 512), 512)
        g1_s[g] = dot(cot_t[theirs, :], attended).astype(BF16)
        send(g1_s.at[g], g1_r.at[g], G1 + g, at_core())
        g_own[g] = dot(cot_t[ours, :], attended).reshape(16, 32, WIDTH)

    def reduce_plane(g):
        take(g1_r.at[g], G1 + g)
        total = g_own[g] + g1_r[g].astype(F32).reshape(16, 32, WIDTH)
        g_own[g] = total
        g2_s[g] = total.astype(BF16)

        def one(i, _):
            c = ring(chunk, i, 16)
            send(g2_s.at[g, c], g2_r.at[g, chunk], G2 + g, at_chunk(c))
            return 0

        lax.fori_loop(1, 16, one, 0)
        g2_r[g, chunk] = jnp.zeros((32, WIDTH), BF16)

    def reduce_z():
        for g in range(2):
            take(g2_r.at[g, pl.ds(0, 15)], G2 + g)
            total = g_own[g, chunk]
            for c in range(16):
                total = total + g2_r[g, c].astype(F32)
            g_sum[g] = total.reshape(4, 8, WIDTH)
        for i in range(4):
            zz = core * 8 + yh * 4 + i
            g3_s[i] = jnp.concatenate([g_sum[0, i], g_sum[1, i]], 0).astype(BF16)

            @pl.when(zz != z)
            def _():
                send(g3_s.at[i], g3_r.at[z], G3, at_p(yl * 16 + zz))

    owner = (lax.div(z, 8) == core) & (lax.rem(lax.div(z, 4), 2) == yh)

    def reduce_last():
        @pl.when(owner)
        def _():
            take(g3_r.at[pl.ds(0, NZ - 1)], G3)
            g3_r[z] = g3_s[lax.rem(z, 4)]
            total = g3_r[0].astype(F32)
            for i in range(1, NZ):
                total = total + g3_r[i].astype(F32)
            g4_s[...] = total
            pl.semaphore_wait(core_sem, 1)
            for c in (1, 2, 3):
                send(g4_s, g4_r, G4, (ring(dp, c, 4), ctx))

    def finish():
        @pl.when(owner)
        def _():
            g4_r[...] = g4_s[...]

        @pl.when(jnp.logical_not(owner))
        def _():
            pl.semaphore_wait(core_sem, 1)
            take(g4_r, G4)

        gw_ref[:, :WIDTH] = g4_r[0:6, :]
        gw_ref[:, WIDTH:] = g4_r[8:14, :]

    load_unpad.wait()
    take(rt_r.at[pl.ds(0, 3)], RT)
    for index, ref in enumerate((att_ref, gq_ref, gk_ref, gv_ref)):
        heads = jnp.concatenate([rt_r[h, index] for h in range(HEADS)], axis=1)
        ref[:, :WIDTH] = dot(heads, unpad_ref[...]).astype(BF16)
    reduce_core(0)
    unpack(3, [((att_ref, WIDTH), (gq_ref, WIDTH))])
    unpack(4, [((att_ref, WIDTH + 128), (att_ref, WIDTH + 256))])
    reduce_core(1)
    reduce_plane(0)
    reduce_plane(1)
    reduce_z()
    exchange(7)
    unpack(5, [((gk_ref, WIDTH), (gv_ref, WIDTH)), ((gq_ref, WIDTH + 128), (gq_ref, WIDTH + 256))])
    reduce_last()
    unpack(6, [((gk_ref, WIDTH + 128), (gk_ref, WIDTH + 256))])
    finish()
    unpack(7, [((gv_ref, WIDTH + 128), (gv_ref, WIDTH + 256))])

    for slot in range(8):
        sent(cs[slot].at[pl.ds(0, GROUP - 1)], slot)
    sent(wz_recv.at[pl.ds(0, NZ - 1)], WZ)
    sent(rs.at[pl.ds(0, 3)], RQ)
    sent(wg.at[core, pl.ds(0, 15)], WX)
    sent(wg.at[core], WC)
    sent(rs_do.at[pl.ds(0, 3)], RD)
    sent(rt_s.at[pl.ds(0, 3)], RT)
    for g in range(2):
        sent(g1_s.at[g], G1 + g)
        sent(g2_s.at[g, pl.ds(0, 15)], G2 + g)

    @pl.when(owner)
    def _():
        sent(g3_s.at[pl.ds(0, 3)], G3)
        sent(g_sum.at[pl.ds(0, 2), pl.ds(0, 3)], G4)

    @pl.when(jnp.logical_not(owner))
    def _():
        sent(g3_s, G3)


def hand_over(*refs):
    n = 4
    srcs, dsts, held, sems = refs[:n], refs[n : 2 * n], refs[2 * n : 3 * n], refs[3 * n]
    inward = [pltpu.make_async_copy(a, b, sems.at[0, i]) for i, (a, b) in enumerate(zip(srcs, held, strict=True))]
    outward = [pltpu.make_async_copy(a, b, sems.at[1, i]) for i, (a, b) in enumerate(zip(held, dsts, strict=True))]
    for copy in inward:
        copy.start()
    for first, second in zip(inward, outward, strict=True):
        first.wait()
        second.start()
    for copy in outward:
        copy.wait()


def body(queries, key_rows, value_rows, out_weight, cotangent, *matrices):
    vmem, hbm = pl.BlockSpec(memory_space=pltpu.VMEM), pl.BlockSpec(memory_space=pltpu.HBM)
    tokens = jax.ShapeDtypeStruct((ROWS, 2 * WIDTH), BF16)
    weight = jax.ShapeDtypeStruct((6, 2 * WIDTH), F32)
    inputs = (queries[0], key_rows[0], value_rows[0], out_weight, cotangent[0], *matrices)
    messages = [pltpu.VMEM((GROUP, 16, 128 * t), BF16) for t in TILES]
    outs = pl.pallas_call(
        kernel,
        out_shape=(tokens, tokens, tokens, weight),
        in_specs=[hbm] * len(inputs),
        out_specs=(vmem,) * 4,
        scratch_shapes=[pltpu.VMEM(a.shape, a.dtype) for a in inputs]
        + [
            pltpu.VMEM((16, 128), F32),
            pltpu.VMEM((16, 128), BF16),
            pltpu.VMEM((NZ, 16, 128), BF16),
            pltpu.VMEM((2, 16, 48, WIDTH), BF16),
            pltpu.VMEM((ROWS, 768), BF16),
            pltpu.VMEM((1024, ROWS), BF16),
            pltpu.VMEM((ROWS, 2 * WIDTH), BF16),
            *messages,
            *messages,
            pltpu.VMEM((ROWS, WIDTH), BF16),
            pltpu.VMEM((ROWS, WIDTH), BF16),
            pltpu.VMEM((ROWS, WIDTH), BF16),
            pltpu.VMEM((ROWS, WIDTH), BF16),
            pltpu.VMEM((HEADS, ROWS, ROWS), F32),
            pltpu.VMEM((HEADS, ROWS, ROWS), BF16),
            pltpu.VMEM((HEADS, ROWS, ROWS), BF16),
            pltpu.VMEM((ROWS, WIDTH), F32),
            pltpu.VMEM((ROWS, WIDTH), F32),
            pltpu.VMEM((ROWS, WIDTH), F32),
            pltpu.VMEM((ROWS, WIDTH), F32),
            pltpu.VMEM((4, 3, ROWS, 128), BF16),
            pltpu.VMEM((4, 3, ROWS, 128), BF16),
            pltpu.VMEM((4, ROWS, 128), BF16),
            pltpu.VMEM((4, ROWS, 128), BF16),
            pltpu.VMEM((4, 4, ROWS, 128), BF16),
            pltpu.VMEM((4, 4, ROWS, 128), BF16),
            pltpu.VMEM((1024, 128), F32),
            pltpu.VMEM((1024, 128), F32),
            pltpu.VMEM((ROWS, 2 * WIDTH), BF16),
            pltpu.VMEM((2, 512, WIDTH), BF16),
            pltpu.VMEM((2, 512, WIDTH), BF16),
            pltpu.VMEM((2, 16, 32, WIDTH), F32),
            pltpu.VMEM((2, 16, 32, WIDTH), BF16),
            pltpu.VMEM((2, 16, 32, WIDTH), BF16),
            pltpu.VMEM((2, 4, 8, WIDTH), F32),
            pltpu.VMEM((4, 16, WIDTH), BF16),
            pltpu.VMEM((NZ, 16, WIDTH), BF16),
            pltpu.VMEM((16, WIDTH), F32),
            pltpu.VMEM((16, WIDTH), F32),
            pltpu.SemaphoreType.DMA((len(inputs),)),
            pltpu.SemaphoreType.DMA((SEMS,)),
            pltpu.SemaphoreType.DMA((SEMS,)),
            pltpu.SemaphoreType.REGULAR,
            pltpu.SemaphoreType.REGULAR,
            pltpu.SemaphoreType.REGULAR,
        ],
        compiler_params=pltpu.CompilerParams(
            collective_id=0, has_side_effects=True, vmem_limit_bytes=60 * 1024 * 1024
        ),
        cost_estimate=pl.CostEstimate(
            flops=8_000_000_000, bytes_accessed=8_000_000, transcendentals=2_000_000
        ),
        name="strided_attention",
    )(*inputs)
    outs = pl.pallas_call(
        hand_over,
        out_shape=(tokens, tokens, tokens, weight),
        in_specs=[hbm] * 4,
        out_specs=(hbm,) * 4,
        scratch_shapes=[pltpu.VMEM(a.shape, a.dtype) for a in outs] + [pltpu.SemaphoreType.DMA((2, 4))],
        name="hand_over",
    )(*outs)
    return (outs[0][None], outs[1][None], outs[2][None], outs[3])


def solution(mesh):
    tokens, rows = P("dp", "ctx", None), P("ctx", None)
    matrices = selections()
    mapped = jax.shard_map(
        body,
        mesh=mesh,
        in_specs=(tokens, tokens, tokens, rows, tokens) + (P(None, None),) * len(matrices),
        out_specs=(tokens, tokens, tokens, rows),
        check_vma=False,
    )

    def run(queries, key_rows, value_rows, out_weight, cotangent):
        return mapped(queries, key_rows, value_rows, out_weight, cotangent, *matrices)

    return run
```

```python
import jax
import jax.numpy as jnp
import numpy as np
from jax import lax
from jax.experimental import pallas as pl
from jax.experimental.pallas import tpu as pltpu
from jax.sharding import PartitionSpec as P

HS = 96
HEADS = 4
WIDTH = HEADS * HS
NX, NZ = 4, 16
GROUP = 32
ROWS = 256
CLASSES = 8
SCALE = HS**-0.5
F32, BF16 = jnp.float32, jnp.bfloat16
NT = (((1,), (1,)), ((), ()))
TN = (((0,), (0,)), ((), ()))


def dot(a, b, dims=None):
    if dims is None:
        return jnp.dot(a, b, preferred_element_type=F32)
    return lax.dot_general(a, b, dims, preferred_element_type=F32)


def selections():
    spread = np.zeros((768, 768), np.float32)
    gather = np.zeros((1024, 768), np.float32)
    for yl in range(2):
        for z in range(NZ):
            for x in range(NX):
                for r in range(6):
                    f = (yl * 64 + z * 4 + x) * 6 + r
                    spread[f, (((r // 3 * 2 + yl) * 4 + x) * 16 + z) * 3 + r % 3] = 1
                    gather[(((z // 8 * 4 + x) * 2 + yl) * 8 + z % 8) * 8 + r, f] = 1
    rows = np.zeros((3, 48, 256), np.float32)
    for t in range(3):
        for z in range(NZ):
            for r in range(3):
                rows[t, z * 3 + r, z * 16 + r * 3 + t] = 1
    pad = np.zeros((WIDTH, 512), np.float32)
    for h in range(HEADS):
        for i in range(HS):
            pad[h * HS + i, h * 128 + i] = 1
    return [jnp.asarray(m, BF16) for m in (spread, gather, rows, pad, pad.T)]


WZ, WX, WC, RQ, RD, RT, G1, G2, G3, G4 = 9, 10, 11, 12, 13, 14, 15, 17, 19, 20
SEMS = 21
TILES = (4, 1, 1, 1, 1, 1, 1, 1, 1)
LAST_ORDER = (0, 1, 2, 3, 4, 15, 5, 14, 6, 13, 7, 12, 8, 9, 10, 11)


def kernel(
    q_hbm, k_hbm, v_hbm, w_hbm, c_hbm, spread_hbm, gather_hbm, rows_hbm, pad_hbm, unpad_hbm,
    gq_ref, gk_ref, gv_ref, gw_ref,
    q_ref, k_ref, v_ref, w_ref, c_ref, spread_ref, gather_ref, rows_ref, pad_ref, unpad_ref,
    wz_rows, wz_send, wz_recv, wg, cot_p, cot_t, go,
    cs0, cs1, cs2, cs3, cs4, cs5, cs6, cs7, cs8, cr0, cr1, cr2, cr3, cr4, cr5, cr6, cr7, cr8,
    qc, kc, vc, dc, probs_ref, half_ref, ds_ref, att_a, dq_a, dk_a, dv_a,
    rs, rr, rs_do, rr_do, rt_s, rt_r, racc_k, racc_v, att_ref,
    g1_s, g1_r, g_own, g2_s, g2_r, g_sum, g3_s, g3_r, g4_s, g4_r,
    isem, ssem, rsem,
):
    cs = (cs0, cs1, cs2, cs3, cs4, cs5, cs6, cs7, cs8)
    cr = (cr0, cr1, cr2, cr3, cr4, cr5, cr6, cr7, cr8)
    dp, ctx = lax.axis_index("dp"), lax.axis_index("ctx")
    core, yh = lax.rem(dp, 2), lax.div(dp, 2)
    x, p = lax.rem(ctx, 4), lax.div(ctx, 4)
    z, yl = lax.rem(p, 16), lax.div(p, 16)
    y = yh * 2 + yl
    chunk = x * 4 + yl * 2 + yh

    loads = [
        pltpu.make_async_copy(src, dst, isem.at[i])
        for i, (src, dst) in enumerate(
            (
                (q_hbm, q_ref), (k_hbm, k_ref), (v_hbm, v_ref), (w_hbm, w_ref), (pad_hbm, pad_ref),
                (c_hbm, c_ref), (spread_hbm, spread_ref), (rows_hbm, rows_ref),
                (gather_hbm, gather_ref), (unpad_hbm, unpad_ref),
            )
        )
    ]
    (load_q, load_k, load_v, load_w, load_pad, load_c, load_spread, load_rows, load_gather,
     load_unpad) = loads
    for load in loads[:4]:
        load.start()

    def at_p(pp):
        return (dp, pp * 4 + x)

    def at_x(xx):
        return (dp, p * 4 + xx)

    def at_y(yy):
        return (lax.div(yy, 2) * 2 + core, lax.rem(yy, 2) * 64 + z * 4 + x)

    def at_chunk(c):
        return (lax.rem(c, 2) * 2 + core, lax.rem(lax.div(c, 2), 2) * 64 + z * 4 + lax.div(c, 4))

    def at_core():
        return (yh * 2 + 1 - core, ctx)

    def ring(i, by, n):
        return lax.rem(i + by, n)

    def send(src, dst, sem, where):
        pltpu.make_async_remote_copy(
            src_ref=src, dst_ref=dst, send_sem=ssem.at[sem], recv_sem=rsem.at[sem],
            device_id=where, device_id_type=pl.DeviceIdType.MESH,
        ).start()

    def take(ref, sem):
        pltpu.make_async_copy(ref, ref, rsem.at[sem]).wait()

    def sent(ref, sem):
        pltpu.make_async_copy(ref, ref, ssem.at[sem]).wait()

    barrier = pltpu.get_barrier_semaphore()

    def greet(where):
        pl.semaphore_signal(barrier, inc=1, device_id=where, device_id_type=pl.DeviceIdType.MESH)

    def greet_p(i, _):
        greet(at_p(ring(p, i, GROUP)))
        return 0

    lax.fori_loop(1, GROUP, greet_p, 0)


    def greet_chunk(i, _):
        greet(at_chunk(ring(chunk, i, 16)))
        return 0

    lax.fori_loop(1, 16, greet_chunk, 0)
    greet(at_core())
    greet(((1 - yh) * 2 + 1 - core, ctx))
    for load in loads[4:]:
        load.start()

    def pack(slot, pairs):
        def one(m, _):
            rows = pl.ds(pl.multiple_of(m * 16, 16), 16)
            for t, ((a_ref, a0), (b_ref, b0)) in enumerate(pairs):
                a = a_ref[rows, a0 : a0 + 128].astype(F32)
                b = b_ref[rows, b0 : b0 + 128].astype(F32)
                lanes = slice(t * 128, (t + 1) * 128)
                cs[slot][2 * m, :, lanes] = jnp.concatenate([a[:8], b[:8]], 0).astype(BF16)
                cs[slot][2 * m + 1, :, lanes] = jnp.concatenate([a[8:], b[8:]], 0).astype(BF16)
            return 0

        lax.fori_loop(0, 16, one, 0)

    def exchange(slot):
        def one(i, _):
            half = lax.div(i + 1, 2)
            odd = lax.rem(i, 2)
            pp = ring(p, odd * half + (1 - odd) * (GROUP - half), GROUP)
            send(cs[slot].at[pp], cr[slot].at[p], slot, at_p(pp))
            return 0

        if slot < len(TILES) - 1:
            lax.fori_loop(1, GROUP, one, 0)
        else:
            for zz in LAST_ORDER:
                for by in range(2):
                    pp = ring(yl, by, 2) * 16 + zz

                    @pl.when(pp != p)
                    def _():
                        send(cs[slot].at[pp], cr[slot].at[p], slot, at_p(pp))

        cr[slot][p] = cs[slot][p]

    def unpack(slot, pairs):
        take(cr[slot].at[pl.ds(0, GROUP - 1)], slot)

        def one(m, _):
            rows = pl.ds(pl.multiple_of(m * 16, 16), 16)
            for t, ((a_ref, a0), (b_ref, b0)) in enumerate(pairs):
                lanes = slice(t * 128, (t + 1) * 128)
                first = cr[slot][2 * m, :, lanes].astype(F32)
                second = cr[slot][2 * m + 1, :, lanes].astype(F32)
                a_ref[rows, a0 : a0 + 128] = jnp.concatenate([first[:8], second[:8]], 0).astype(BF16)
                b_ref[rows, b0 : b0 + 128] = jnp.concatenate([first[8:], second[8:]], 0).astype(BF16)
            return 0

        lax.fori_loop(0, 16, one, 0)

    load_q.wait()
    load_k.wait()
    load_v.wait()
    pack(
        0,
        [((q_ref, WIDTH + t), (k_ref, WIDTH + t)) for t in (0, 128, 256)]
        + [((v_ref, WIDTH), (v_ref, WIDTH + 128))],
    )
    load_w.wait()
    w = w_ref[...].astype(F32)
    w = jnp.where(core == 0, w[:, :WIDTH], w[:, WIDTH:])
    w = jnp.where(yh == 0, w[0:3], w[3:6])
    wz_rows[...] = jnp.zeros((16, 128), F32)
    for r in range(3):
        for t in range(3):
            wz_rows[r * 3 + t : r * 3 + t + 1, :] = w[r : r + 1, t * 128 : (t + 1) * 128]
    wz_send[...] = wz_rows[...].astype(BF16)
    wz_recv[z] = wz_send[...]
    pl.semaphore_wait(barrier, 48)

    def send_w(i, _):
        send(wz_send, wz_recv.at[z], WZ, at_p(yl * 16 + ring(z, i, NZ)))
        return 0

    lax.fori_loop(1, NZ, send_w, 0)
    exchange(0)

    load_pad.wait()
    for index, ref in enumerate((q_ref, k_ref, v_ref)):
        padded = dot(ref[:, :WIDTH], pad_ref[...]).astype(BF16)
        for h in range(HEADS):
            rs[h, index] = padded[:, h * 128 : (h + 1) * 128]
    for i in range(1, 4):
        xx = ring(x, i, 4)
        send(rs.at[xx], rr.at[x], RQ, at_x(xx))
    rr[x] = rs[x]

    load_rows.wait()
    take(wz_recv.at[pl.ds(0, NZ - 1)], WZ)
    at = yh * 8 + yl * 4 + x
    gathered = wz_recv[...].reshape(256, 128)
    for t in range(3):
        wg[core, at, :, t * 128 : (t + 1) * 128] = dot(rows_ref[t], gathered).astype(BF16)
    own = wg.at[core, at]

    def send_plane(i, _):
        send(own, own, WX, at_chunk(ring(chunk, i, 16)))
        return 0

    lax.fori_loop(1, 16, send_plane, 0)

    load_c.wait()
    load_spread.wait()
    cot_p[...] = dot(c_ref[...], spread_ref[...]).astype(BF16)

    load_gather.wait()
    cot_t[...] = dot(gather_ref[...], c_ref[...], NT).astype(BF16)
    take(wg.at[core, pl.ds(0, 15)], WX)
    send(wg.at[core], wg.at[core], WC, at_core())
    take(wg.at[1 - core], WC)

    def grad_out(c):
        go[:, c * WIDTH : (c + 1) * WIDTH] = dot(
            cot_p[...], wg[c].reshape(768, WIDTH)
        ).astype(BF16)

    grad_out(1)
    pack(1, [((go, WIDTH), (go, WIDTH + 128))])
    exchange(1)
    pack(2, [((go, WIDTH + 256), (v_ref, WIDTH + 256))])
    exchange(2)
    grad_out(0)
    padded = dot(go[:, :WIDTH], pad_ref[...]).astype(BF16)
    for h in range(HEADS):
        rs_do[h] = padded[:, h * 128 : (h + 1) * 128]
    for i in range(1, 4):
        xx = ring(x, i, 4)
        send(rs_do.at[xx], rr_do.at[x], RD, at_x(xx))
    rr_do[x] = rs_do[x]

    unpack(0, [((qc, t), (kc, t)) for t in (0, 128, 256)] + [((vc, 0), (vc, 128))])
    row_at = lax.broadcasted_iota(jnp.int32, (ROWS, ROWS), 0)
    key_at = lax.broadcasted_iota(jnp.int32, (ROWS, ROWS), 1)
    lanes = lax.broadcasted_iota(jnp.int32, (ROWS, WIDTH), 1)

    def span(h):
        return h * HS // 128 * 128, -(-(h + 1) * HS // 128) * 128

    def head(ref, h):
        lo, hi = span(h)
        at = lanes[:, lo:hi]
        value = ref[:, lo:hi]
        return jnp.where((at >= h * HS) & (at < (h + 1) * HS), value, jnp.zeros_like(value))

    def put(ref, h, value):
        lo, hi = span(h)
        for t in range(lo, hi, 128):
            if h > 0 and t == lo:
                ref[:, t : t + 128] += value[:, t - lo : t - lo + 128]
            else:
                ref[:, t : t + 128] = value[:, t - lo : t - lo + 128]

    def softmax(scores):
        top = jnp.max(scores, axis=1, keepdims=True)
        total = top + jnp.log(jnp.sum(jnp.exp(scores - top), axis=1, keepdims=True))
        return jnp.exp(scores - total)

    for h in range(HEADS):
        lo, hi = span(h)
        scores = dot(head(qc, h), kc[:, lo:hi], NT) * SCALE
        allowed = (key_at <= row_at) & (lax.rem(row_at - key_at, CLASSES) == 0)
        probs = softmax(jnp.where(allowed, scores, -1e30))
        probs_ref[h] = probs
        half_ref[h] = probs.astype(BF16)

    take(rr.at[pl.ds(0, 3)], RQ)
    take(rr_do.at[pl.ds(0, 3)], RD)
    racc_k[...] = jnp.zeros_like(racc_k)
    racc_v[...] = jnp.zeros_like(racc_v)
    for i in range(4):
        n = (i + 1) * ROWS
        query, out = rr[i, 0], rr_do[i]
        keys = rr[0 : i + 1, 1].reshape(n, 128)
        values = rr[0 : i + 1, 2].reshape(n, 128)
        at = lax.broadcasted_iota(jnp.int32, (ROWS, n), 0) + i * ROWS
        allowed = lax.broadcasted_iota(jnp.int32, (ROWS, n), 1) <= at
        probs = softmax(jnp.where(allowed, dot(query, keys, NT) * SCALE, -1e30))
        half = probs.astype(BF16)
        attended = dot(half, values).astype(BF16)
        deltas = jnp.sum(out.astype(F32) * attended.astype(F32), axis=1, keepdims=True)
        dscores = (probs * (dot(out, values, NT) - deltas) * SCALE).astype(BF16)
        rt_s[i, 0] = attended
        rt_s[i, 1] = dot(dscores, keys).astype(BF16)
        racc_k[0:n, :] += dot(dscores, query, TN)
        racc_v[0:n, :] += dot(half, out, TN)
    for i in range(4):
        rt_s[i, 2] = racc_k[i * ROWS : (i + 1) * ROWS, :].astype(BF16)
        rt_s[i, 3] = racc_v[i * ROWS : (i + 1) * ROWS, :].astype(BF16)
    for i in range(1, 4):
        xx = ring(x, i, 4)
        send(rt_s.at[xx], rt_r.at[x], RT, at_x(xx))
    rt_r[x] = rt_s[x]

    def attend(h):
        put(att_a, h, dot(half_ref[h], head(vc, h)).astype(BF16).astype(F32))

    def score_grads(h):
        lo, hi = span(h)
        out = head(dc, h)
        deltas = jnp.sum(out.astype(F32) * att_a[:, lo:hi], axis=1, keepdims=True)
        dprobs = dot(out, vc[:, lo:hi], NT)
        dscores = (probs_ref[h] * (dprobs - deltas) * SCALE).astype(BF16)
        ds_ref[h] = dscores
        put(dq_a, h, dot(dscores, head(kc, h)))

    def key_grads(h):
        put(dk_a, h, dot(ds_ref[h], head(qc, h), TN))
        put(dv_a, h, dot(half_ref[h], head(dc, h), TN))

    unpack(1, [((dc, 0), (dc, 128))])
    for h in (0, 1):
        attend(h)
        score_grads(h)
    pack(3, [((att_a, 0), (dq_a, 0))])
    exchange(3)
    for h in (0, 1):
        key_grads(h)
    unpack(2, [((dc, 256), (vc, 256))])
    for h in (2, 3):
        attend(h)
    pack(4, [((att_a, 128), (att_a, 256))])
    exchange(4)
    pack(5, [((dk_a, 0), (dv_a, 0))])
    exchange(5)
    for h in (2, 3):
        score_grads(h)
        key_grads(h)
    pack(6, [((dq_a, 128), (dq_a, 256))])
    pack(7, [((dk_a, 128), (dk_a, 256))])
    pack(8, [((dv_a, 128), (dv_a, 256))])

    def reduce_core(g):
        attended = att_ref[:, g * WIDTH : (g + 1) * WIDTH]
        theirs = pl.ds(pl.multiple_of((1 - core) * 512, 512), 512)
        ours = pl.ds(pl.multiple_of(core * 512, 512), 512)
        g1_s[g] = dot(cot_t[theirs, :], attended).astype(BF16)
        send(g1_s.at[g], g1_r.at[g], G1 + g, at_core())
        g_own[g] = dot(cot_t[ours, :], attended).reshape(16, 32, WIDTH)

    def reduce_plane(g):
        take(g1_r.at[g], G1 + g)
        total = g_own[g] + g1_r[g].astype(F32).reshape(16, 32, WIDTH)
        g_own[g] = total
        g2_s[g] = total.astype(BF16)

        def one(i, _):
            c = ring(chunk, i, 16)
            send(g2_s.at[g, c], g2_r.at[g, chunk], G2 + g, at_chunk(c))
            return 0

        lax.fori_loop(1, 16, one, 0)
        g2_r[g, chunk] = jnp.zeros((32, WIDTH), BF16)

    def reduce_z():
        for g in range(2):
            take(g2_r.at[g, pl.ds(0, 15)], G2 + g)
            total = g_own[g, chunk]
            for c in range(16):
                total = total + g2_r[g, c].astype(F32)
            g_sum[g] = total.reshape(4, 8, WIDTH)
        for i in range(4):
            zz = core * 8 + yh * 4 + i
            g3_s[i] = jnp.concatenate([g_sum[0, i], g_sum[1, i]], 0).astype(BF16)

            @pl.when(zz != z)
            def _():
                send(g3_s.at[i], g3_r.at[z], G3, at_p(yl * 16 + zz))

    owner = (lax.div(z, 8) == core) & (lax.rem(lax.div(z, 4), 2) == yh)

    def reduce_last():
        @pl.when(owner)
        def _():
            take(g3_r.at[pl.ds(0, NZ - 1)], G3)
            g3_r[z] = g3_s[lax.rem(z, 4)]
            total = g3_r[0].astype(F32)
            for i in range(1, NZ):
                total = total + g3_r[i].astype(F32)
            g4_s[...] = total
            for c in (1, 2, 3):
                send(g4_s, g4_r, G4, (ring(dp, c, 4), ctx))

    def finish():
        @pl.when(owner)
        def _():
            g4_r[...] = g4_s[...]

        @pl.when(jnp.logical_not(owner))
        def _():
            take(g4_r, G4)

        gw_ref[:, :WIDTH] = g4_r[0:6, :]
        gw_ref[:, WIDTH:] = g4_r[8:14, :]

    load_unpad.wait()
    take(rt_r.at[pl.ds(0, 3)], RT)
    for index, ref in enumerate((att_ref, gq_ref, gk_ref, gv_ref)):
        heads = jnp.concatenate([rt_r[h, index] for h in range(HEADS)], axis=1)
        ref[:, :WIDTH] = dot(heads, unpad_ref[...]).astype(BF16)
    reduce_core(0)
    reduce_plane(0)
    unpack(3, [((att_ref, WIDTH), (gq_ref, WIDTH))])
    unpack(4, [((att_ref, WIDTH + 128), (att_ref, WIDTH + 256))])
    reduce_core(1)
    exchange(6)
    exchange(7)
    reduce_plane(1)
    reduce_z()
    exchange(8)
    unpack(5, [((gk_ref, WIDTH), (gv_ref, WIDTH))])
    unpack(6, [((gq_ref, WIDTH + 128), (gq_ref, WIDTH + 256))])
    unpack(7, [((gk_ref, WIDTH + 128), (gk_ref, WIDTH + 256))])
    reduce_last()
    unpack(8, [((gv_ref, WIDTH + 128), (gv_ref, WIDTH + 256))])
    finish()

    for slot in range(9):
        sent(cs[slot].at[pl.ds(0, GROUP - 1)], slot)
    sent(wz_recv.at[pl.ds(0, NZ - 1)], WZ)
    sent(rs.at[pl.ds(0, 3)], RQ)
    sent(wg.at[core, pl.ds(0, 15)], WX)
    sent(wg.at[core], WC)
    sent(rs_do.at[pl.ds(0, 3)], RD)
    sent(rt_s.at[pl.ds(0, 3)], RT)
    for g in range(2):
        sent(g1_s.at[g], G1 + g)
        sent(g2_s.at[g, pl.ds(0, 15)], G2 + g)

    @pl.when(owner)
    def _():
        sent(g3_s.at[pl.ds(0, 3)], G3)
        sent(g_sum.at[pl.ds(0, 2), pl.ds(0, 3)], G4)

    @pl.when(jnp.logical_not(owner))
    def _():
        sent(g3_s, G3)


def hand_over(*refs):
    n = 4
    srcs, dsts, held, sems = refs[:n], refs[n : 2 * n], refs[2 * n : 3 * n], refs[3 * n]
    inward = [pltpu.make_async_copy(a, b, sems.at[0, i]) for i, (a, b) in enumerate(zip(srcs, held, strict=True))]
    outward = [pltpu.make_async_copy(a, b, sems.at[1, i]) for i, (a, b) in enumerate(zip(held, dsts, strict=True))]
    for copy in inward:
        copy.start()
    for first, second in zip(inward, outward, strict=True):
        first.wait()
        second.start()
    for copy in outward:
        copy.wait()


def body(queries, key_rows, value_rows, out_weight, cotangent, *matrices):
    vmem, hbm = pl.BlockSpec(memory_space=pltpu.VMEM), pl.BlockSpec(memory_space=pltpu.HBM)
    tokens = jax.ShapeDtypeStruct((ROWS, 2 * WIDTH), BF16)
    weight = jax.ShapeDtypeStruct((6, 2 * WIDTH), F32)
    inputs = (queries[0], key_rows[0], value_rows[0], out_weight, cotangent[0], *matrices)
    messages = [pltpu.VMEM((GROUP, 16, 128 * t), BF16) for t in TILES]
    outs = pl.pallas_call(
        kernel,
        out_shape=(tokens, tokens, tokens, weight),
        in_specs=[hbm] * len(inputs),
        out_specs=(vmem,) * 4,
        scratch_shapes=[pltpu.VMEM(a.shape, a.dtype) for a in inputs]
        + [
            pltpu.VMEM((16, 128), F32),
            pltpu.VMEM((16, 128), BF16),
            pltpu.VMEM((NZ, 16, 128), BF16),
            pltpu.VMEM((2, 16, 48, WIDTH), BF16),
            pltpu.VMEM((ROWS, 768), BF16),
            pltpu.VMEM((1024, ROWS), BF16),
            pltpu.VMEM((ROWS, 2 * WIDTH), BF16),
            *messages,
            *messages,
            pltpu.VMEM((ROWS, WIDTH), BF16),
            pltpu.VMEM((ROWS, WIDTH), BF16),
            pltpu.VMEM((ROWS, WIDTH), BF16),
            pltpu.VMEM((ROWS, WIDTH), BF16),
            pltpu.VMEM((HEADS, ROWS, ROWS), F32),
            pltpu.VMEM((HEADS, ROWS, ROWS), BF16),
            pltpu.VMEM((HEADS, ROWS, ROWS), BF16),
            pltpu.VMEM((ROWS, WIDTH), F32),
            pltpu.VMEM((ROWS, WIDTH), F32),
            pltpu.VMEM((ROWS, WIDTH), F32),
            pltpu.VMEM((ROWS, WIDTH), F32),
            pltpu.VMEM((4, 3, ROWS, 128), BF16),
            pltpu.VMEM((4, 3, ROWS, 128), BF16),
            pltpu.VMEM((4, ROWS, 128), BF16),
            pltpu.VMEM((4, ROWS, 128), BF16),
            pltpu.VMEM((4, 4, ROWS, 128), BF16),
            pltpu.VMEM((4, 4, ROWS, 128), BF16),
            pltpu.VMEM((1024, 128), F32),
            pltpu.VMEM((1024, 128), F32),
            pltpu.VMEM((ROWS, 2 * WIDTH), BF16),
            pltpu.VMEM((2, 512, WIDTH), BF16),
            pltpu.VMEM((2, 512, WIDTH), BF16),
            pltpu.VMEM((2, 16, 32, WIDTH), F32),
            pltpu.VMEM((2, 16, 32, WIDTH), BF16),
            pltpu.VMEM((2, 16, 32, WIDTH), BF16),
            pltpu.VMEM((2, 4, 8, WIDTH), F32),
            pltpu.VMEM((4, 16, WIDTH), BF16),
            pltpu.VMEM((NZ, 16, WIDTH), BF16),
            pltpu.VMEM((16, WIDTH), F32),
            pltpu.VMEM((16, WIDTH), F32),
            pltpu.SemaphoreType.DMA((len(inputs),)),
            pltpu.SemaphoreType.DMA((SEMS,)),
            pltpu.SemaphoreType.DMA((SEMS,)),
        ],
        compiler_params=pltpu.CompilerParams(
            collective_id=0, has_side_effects=True, vmem_limit_bytes=60 * 1024 * 1024
        ),
        cost_estimate=pl.CostEstimate(
            flops=8_000_000_000, bytes_accessed=8_000_000, transcendentals=2_000_000
        ),
        name="strided_attention",
    )(*inputs)
    outs = pl.pallas_call(
        hand_over,
        out_shape=(tokens, tokens, tokens, weight),
        in_specs=[hbm] * 4,
        out_specs=(hbm,) * 4,
        scratch_shapes=[pltpu.VMEM(a.shape, a.dtype) for a in outs] + [pltpu.SemaphoreType.DMA((2, 4))],
        name="hand_over",
    )(*outs)
    return (outs[0][None], outs[1][None], outs[2][None], outs[3])


def solution(mesh):
    tokens, rows = P("dp", "ctx", None), P("ctx", None)
    matrices = selections()
    mapped = jax.shard_map(
        body,
        mesh=mesh,
        in_specs=(tokens, tokens, tokens, rows, tokens) + (P(None, None),) * len(matrices),
        out_specs=(tokens, tokens, tokens, rows),
        check_vma=False,
    )

    def run(queries, key_rows, value_rows, out_weight, cotangent):
        return mapped(queries, key_rows, value_rows, out_weight, cotangent, *matrices)

    return run
```

```python
import jax
import jax.numpy as jnp
import numpy as np
from jax import lax
from jax.experimental import pallas as pl
from jax.experimental.pallas import tpu as pltpu
from jax.sharding import PartitionSpec as P

HS = 96
HEADS = 4
WIDTH = HEADS * HS
NX, NZ = 4, 16
GROUP = 32
ROWS = 256
CLASSES = 8
SCALE = HS**-0.5
F32, BF16 = jnp.float32, jnp.bfloat16
NT = (((1,), (1,)), ((), ()))
TN = (((0,), (0,)), ((), ()))


def dot(a, b, dims=None):
    if dims is None:
        return jnp.dot(a, b, preferred_element_type=F32)
    return lax.dot_general(a, b, dims, preferred_element_type=F32)


def selections():
    spread = np.zeros((768, 768), np.float32)
    gather = np.zeros((1024, 768), np.float32)
    for yl in range(2):
        for z in range(NZ):
            for x in range(NX):
                for r in range(6):
                    f = (yl * 64 + z * 4 + x) * 6 + r
                    spread[f, (((r // 3 * 2 + yl) * 4 + x) * 16 + z) * 3 + r % 3] = 1
                    gather[(((z // 8 * 4 + x) * 2 + yl) * 8 + z % 8) * 8 + r, f] = 1
    rows = np.zeros((3, 48, 256), np.float32)
    for t in range(3):
        for z in range(NZ):
            for r in range(3):
                rows[t, z * 3 + r, z * 16 + r * 3 + t] = 1
    pad = np.zeros((WIDTH, 512), np.float32)
    for h in range(HEADS):
        for i in range(HS):
            pad[h * HS + i, h * 128 + i] = 1
    return [jnp.asarray(m, BF16) for m in (spread, gather, rows, pad, pad.T)]


WZ, WX, WC, RQ, RD, RT, G1, G2, G3, G4 = 9, 10, 11, 12, 13, 14, 15, 17, 19, 20
SEMS = 21
TILES = (4, 1, 1, 1, 1, 1, 1, 1, 1)
LAST_ORDER = (0, 1, 2, 3, 4, 15, 5, 14, 6, 13, 7, 12, 8, 9, 10, 11)


def kernel(
    q_hbm, k_hbm, v_hbm, w_hbm, c_hbm, spread_hbm, gather_hbm, rows_hbm, pad_hbm, unpad_hbm,
    gq_hbm, gk_hbm, gv_hbm, gw_hbm,
    q_ref, k_ref, v_ref, w_ref, c_ref, spread_ref, gather_ref, rows_ref, pad_ref, unpad_ref,
    wz_rows, wz_send, wz_recv, wg, cot_p, cot_t, go,
    cs0, cs1, cs2, cs3, cs4, cs5, cs6, cs7, cs8, cr0, cr1, cr2, cr3, cr4, cr5, cr6, cr7, cr8,
    qc, kc, vc, dc, probs_ref, half_ref, ds_ref, att_a, dq_a, dk_a, dv_a,
    rs, rr, rs_do, rr_do, rt_s, rt_r, racc_k, racc_v, att_ref,
    g1_s, g1_r, g_own, g2_s, g2_r, g_sum, g3_s, g3_r, g4_s, g4_r,
    gq_ref, gk_ref, gv_ref, gw_ref, osem, isem, ssem, rsem,
):
    cs = (cs0, cs1, cs2, cs3, cs4, cs5, cs6, cs7, cs8)
    cr = (cr0, cr1, cr2, cr3, cr4, cr5, cr6, cr7, cr8)
    dp, ctx = lax.axis_index("dp"), lax.axis_index("ctx")
    core, yh = lax.rem(dp, 2), lax.div(dp, 2)
    x, p = lax.rem(ctx, 4), lax.div(ctx, 4)
    z, yl = lax.rem(p, 16), lax.div(p, 16)
    y = yh * 2 + yl
    chunk = x * 4 + yl * 2 + yh

    loads = [
        pltpu.make_async_copy(src, dst, isem.at[i])
        for i, (src, dst) in enumerate(
            (
                (q_hbm, q_ref), (k_hbm, k_ref), (v_hbm, v_ref), (w_hbm, w_ref), (pad_hbm, pad_ref),
                (c_hbm, c_ref), (spread_hbm, spread_ref), (rows_hbm, rows_ref),
                (gather_hbm, gather_ref), (unpad_hbm, unpad_ref),
            )
        )
    ]
    (load_q, load_k, load_v, load_w, load_pad, load_c, load_spread, load_rows, load_gather,
     load_unpad) = loads
    for load in loads[:4]:
        load.start()

    stores = [
        pltpu.make_async_copy(src, dst, osem.at[i])
        for i, (src, dst) in enumerate(
            ((gq_ref, gq_hbm), (gk_ref, gk_hbm), (gv_ref, gv_hbm), (gw_ref, gw_hbm))
        )
    ]

    def at_p(pp):
        return (dp, pp * 4 + x)

    def at_x(xx):
        return (dp, p * 4 + xx)

    def at_y(yy):
        return (lax.div(yy, 2) * 2 + core, lax.rem(yy, 2) * 64 + z * 4 + x)

    def at_chunk(c):
        return (lax.rem(c, 2) * 2 + core, lax.rem(lax.div(c, 2), 2) * 64 + z * 4 + lax.div(c, 4))

    def at_core():
        return (yh * 2 + 1 - core, ctx)

    def ring(i, by, n):
        return lax.rem(i + by, n)

    def send(src, dst, sem, where):
        pltpu.make_async_remote_copy(
            src_ref=src, dst_ref=dst, send_sem=ssem.at[sem], recv_sem=rsem.at[sem],
            device_id=where, device_id_type=pl.DeviceIdType.MESH,
        ).start()

    def take(ref, sem):
        pltpu.make_async_copy(ref, ref, rsem.at[sem]).wait()

    def sent(ref, sem):
        pltpu.make_async_copy(ref, ref, ssem.at[sem]).wait()

    barrier = pltpu.get_barrier_semaphore()

    def greet(where):
        pl.semaphore_signal(barrier, inc=1, device_id=where, device_id_type=pl.DeviceIdType.MESH)

    def greet_p(i, _):
        greet(at_p(ring(p, i, GROUP)))
        return 0

    lax.fori_loop(1, GROUP, greet_p, 0)


    def greet_chunk(i, _):
        greet(at_chunk(ring(chunk, i, 16)))
        return 0

    lax.fori_loop(1, 16, greet_chunk, 0)
    greet(at_core())
    greet(((1 - yh) * 2 + 1 - core, ctx))
    for load in loads[4:]:
        load.start()

    def pack(slot, pairs):
        def one(m, _):
            rows = pl.ds(pl.multiple_of(m * 16, 16), 16)
            for t, ((a_ref, a0), (b_ref, b0)) in enumerate(pairs):
                a = a_ref[rows, a0 : a0 + 128].astype(F32)
                b = b_ref[rows, b0 : b0 + 128].astype(F32)
                lanes = slice(t * 128, (t + 1) * 128)
                cs[slot][2 * m, :, lanes] = jnp.concatenate([a[:8], b[:8]], 0).astype(BF16)
                cs[slot][2 * m + 1, :, lanes] = jnp.concatenate([a[8:], b[8:]], 0).astype(BF16)
            return 0

        lax.fori_loop(0, 16, one, 0)

    def exchange(slot):
        def one(i, _):
            half = lax.div(i + 1, 2)
            odd = lax.rem(i, 2)
            pp = ring(p, odd * half + (1 - odd) * (GROUP - half), GROUP)
            send(cs[slot].at[pp], cr[slot].at[p], slot, at_p(pp))
            return 0

        if slot < len(TILES) - 1:
            lax.fori_loop(1, GROUP, one, 0)
        else:
            for zz in LAST_ORDER:
                for by in range(2):
                    pp = ring(yl, by, 2) * 16 + zz

                    @pl.when(pp != p)
                    def _():
                        send(cs[slot].at[pp], cr[slot].at[p], slot, at_p(pp))

        cr[slot][p] = cs[slot][p]

    def unpack(slot, pairs):
        take(cr[slot].at[pl.ds(0, GROUP - 1)], slot)

        def one(m, _):
            rows = pl.ds(pl.multiple_of(m * 16, 16), 16)
            for t, ((a_ref, a0), (b_ref, b0)) in enumerate(pairs):
                lanes = slice(t * 128, (t + 1) * 128)
                first = cr[slot][2 * m, :, lanes].astype(F32)
                second = cr[slot][2 * m + 1, :, lanes].astype(F32)
                a_ref[rows, a0 : a0 + 128] = jnp.concatenate([first[:8], second[:8]], 0).astype(BF16)
                b_ref[rows, b0 : b0 + 128] = jnp.concatenate([first[8:], second[8:]], 0).astype(BF16)
            return 0

        lax.fori_loop(0, 16, one, 0)

    load_q.wait()
    load_k.wait()
    load_v.wait()
    pack(
        0,
        [((q_ref, WIDTH + t), (k_ref, WIDTH + t)) for t in (0, 128, 256)]
        + [((v_ref, WIDTH), (v_ref, WIDTH + 128))],
    )
    load_w.wait()
    w = w_ref[...].astype(F32)
    w = jnp.where(core == 0, w[:, :WIDTH], w[:, WIDTH:])
    w = jnp.where(yh == 0, w[0:3], w[3:6])
    wz_rows[...] = jnp.zeros((16, 128), F32)
    for r in range(3):
        for t in range(3):
            wz_rows[r * 3 + t : r * 3 + t + 1, :] = w[r : r + 1, t * 128 : (t + 1) * 128]
    wz_send[...] = wz_rows[...].astype(BF16)
    wz_recv[z] = wz_send[...]
    pl.semaphore_wait(barrier, 48)

    def send_w(i, _):
        send(wz_send, wz_recv.at[z], WZ, at_p(yl * 16 + ring(z, i, NZ)))
        return 0

    lax.fori_loop(1, NZ, send_w, 0)
    exchange(0)

    load_pad.wait()
    for index, ref in enumerate((q_ref, k_ref, v_ref)):
        padded = dot(ref[:, :WIDTH], pad_ref[...]).astype(BF16)
        for h in range(HEADS):
            rs[h, index] = padded[:, h * 128 : (h + 1) * 128]
    for i in range(1, 4):
        xx = ring(x, i, 4)
        send(rs.at[xx], rr.at[x], RQ, at_x(xx))
    rr[x] = rs[x]

    load_rows.wait()
    take(wz_recv.at[pl.ds(0, NZ - 1)], WZ)
    at = yh * 8 + yl * 4 + x
    gathered = wz_recv[...].reshape(256, 128)
    for t in range(3):
        wg[core, at, :, t * 128 : (t + 1) * 128] = dot(rows_ref[t], gathered).astype(BF16)
    own = wg.at[core, at]

    def send_plane(i, _):
        send(own, own, WX, at_chunk(ring(chunk, i, 16)))
        return 0

    lax.fori_loop(1, 16, send_plane, 0)

    load_c.wait()
    load_spread.wait()
    cot_p[...] = dot(c_ref[...], spread_ref[...]).astype(BF16)

    load_gather.wait()
    cot_t[...] = dot(gather_ref[...], c_ref[...], NT).astype(BF16)
    take(wg.at[core, pl.ds(0, 15)], WX)
    send(wg.at[core], wg.at[core], WC, at_core())
    take(wg.at[1 - core], WC)

    def grad_out(c):
        go[:, c * WIDTH : (c + 1) * WIDTH] = dot(
            cot_p[...], wg[c].reshape(768, WIDTH)
        ).astype(BF16)

    grad_out(1)
    pack(1, [((go, WIDTH), (go, WIDTH + 128))])
    exchange(1)
    pack(2, [((go, WIDTH + 256), (v_ref, WIDTH + 256))])
    exchange(2)
    grad_out(0)
    padded = dot(go[:, :WIDTH], pad_ref[...]).astype(BF16)
    for h in range(HEADS):
        rs_do[h] = padded[:, h * 128 : (h + 1) * 128]
    for i in range(1, 4):
        xx = ring(x, i, 4)
        send(rs_do.at[xx], rr_do.at[x], RD, at_x(xx))
    rr_do[x] = rs_do[x]

    unpack(0, [((qc, t), (kc, t)) for t in (0, 128, 256)] + [((vc, 0), (vc, 128))])
    row_at = lax.broadcasted_iota(jnp.int32, (ROWS, ROWS), 0)
    key_at = lax.broadcasted_iota(jnp.int32, (ROWS, ROWS), 1)
    lanes = lax.broadcasted_iota(jnp.int32, (ROWS, WIDTH), 1)

    def span(h):
        return h * HS // 128 * 128, -(-(h + 1) * HS // 128) * 128

    def head(ref, h):
        lo, hi = span(h)
        at = lanes[:, lo:hi]
        value = ref[:, lo:hi]
        return jnp.where((at >= h * HS) & (at < (h + 1) * HS), value, jnp.zeros_like(value))

    def put(ref, h, value):
        lo, hi = span(h)
        for t in range(lo, hi, 128):
            if h > 0 and t == lo:
                ref[:, t : t + 128] += value[:, t - lo : t - lo + 128]
            else:
                ref[:, t : t + 128] = value[:, t - lo : t - lo + 128]

    def softmax(scores):
        top = jnp.max(scores, axis=1, keepdims=True)
        total = top + jnp.log(jnp.sum(jnp.exp(scores - top), axis=1, keepdims=True))
        return jnp.exp(scores - total)

    for h in range(HEADS):
        lo, hi = span(h)
        scores = dot(head(qc, h), kc[:, lo:hi], NT) * SCALE
        allowed = (key_at <= row_at) & (lax.rem(row_at - key_at, CLASSES) == 0)
        probs = softmax(jnp.where(allowed, scores, -1e30))
        probs_ref[h] = probs
        half_ref[h] = probs.astype(BF16)

    take(rr.at[pl.ds(0, 3)], RQ)
    take(rr_do.at[pl.ds(0, 3)], RD)
    racc_k[...] = jnp.zeros_like(racc_k)
    racc_v[...] = jnp.zeros_like(racc_v)
    for i in range(4):
        n = (i + 1) * ROWS
        query, out = rr[i, 0], rr_do[i]
        keys = rr[0 : i + 1, 1].reshape(n, 128)
        values = rr[0 : i + 1, 2].reshape(n, 128)
        at = lax.broadcasted_iota(jnp.int32, (ROWS, n), 0) + i * ROWS
        allowed = lax.broadcasted_iota(jnp.int32, (ROWS, n), 1) <= at
        probs = softmax(jnp.where(allowed, dot(query, keys, NT) * SCALE, -1e30))
        half = probs.astype(BF16)
        attended = dot(half, values).astype(BF16)
        deltas = jnp.sum(out.astype(F32) * attended.astype(F32), axis=1, keepdims=True)
        dscores = (probs * (dot(out, values, NT) - deltas) * SCALE).astype(BF16)
        rt_s[i, 0] = attended
        rt_s[i, 1] = dot(dscores, keys).astype(BF16)
        racc_k[0:n, :] += dot(dscores, query, TN)
        racc_v[0:n, :] += dot(half, out, TN)
    for i in range(4):
        rt_s[i, 2] = racc_k[i * ROWS : (i + 1) * ROWS, :].astype(BF16)
        rt_s[i, 3] = racc_v[i * ROWS : (i + 1) * ROWS, :].astype(BF16)
    for i in range(1, 4):
        xx = ring(x, i, 4)
        send(rt_s.at[xx], rt_r.at[x], RT, at_x(xx))
    rt_r[x] = rt_s[x]

    def attend(h):
        put(att_a, h, dot(half_ref[h], head(vc, h)).astype(BF16).astype(F32))

    def score_grads(h):
        lo, hi = span(h)
        out = head(dc, h)
        deltas = jnp.sum(out.astype(F32) * att_a[:, lo:hi], axis=1, keepdims=True)
        dprobs = dot(out, vc[:, lo:hi], NT)
        dscores = (probs_ref[h] * (dprobs - deltas) * SCALE).astype(BF16)
        ds_ref[h] = dscores
        put(dq_a, h, dot(dscores, head(kc, h)))

    def key_grads(h):
        put(dk_a, h, dot(ds_ref[h], head(qc, h), TN))
        put(dv_a, h, dot(half_ref[h], head(dc, h), TN))

    unpack(1, [((dc, 0), (dc, 128))])
    for h in (0, 1):
        attend(h)
        score_grads(h)
    pack(3, [((att_a, 0), (dq_a, 0))])
    exchange(3)
    for h in (0, 1):
        key_grads(h)
    unpack(2, [((dc, 256), (vc, 256))])
    for h in (2, 3):
        attend(h)
    pack(4, [((att_a, 128), (att_a, 256))])
    exchange(4)
    pack(5, [((dk_a, 0), (dv_a, 0))])
    exchange(5)
    for h in (2, 3):
        score_grads(h)
        key_grads(h)
    pack(6, [((dq_a, 128), (dq_a, 256))])
    pack(7, [((dk_a, 128), (dk_a, 256))])
    pack(8, [((dv_a, 128), (dv_a, 256))])

    def reduce_core(g):
        attended = att_ref[:, g * WIDTH : (g + 1) * WIDTH]
        theirs = pl.ds(pl.multiple_of((1 - core) * 512, 512), 512)
        ours = pl.ds(pl.multiple_of(core * 512, 512), 512)
        g1_s[g] = dot(cot_t[theirs, :], attended).astype(BF16)
        send(g1_s.at[g], g1_r.at[g], G1 + g, at_core())
        g_own[g] = dot(cot_t[ours, :], attended).reshape(16, 32, WIDTH)

    def reduce_plane(g):
        take(g1_r.at[g], G1 + g)
        total = g_own[g] + g1_r[g].astype(F32).reshape(16, 32, WIDTH)
        g_own[g] = total
        g2_s[g] = total.astype(BF16)

        def one(i, _):
            c = ring(chunk, i, 16)
            send(g2_s.at[g, c], g2_r.at[g, chunk], G2 + g, at_chunk(c))
            return 0

        lax.fori_loop(1, 16, one, 0)
        g2_r[g, chunk] = jnp.zeros((32, WIDTH), BF16)

    def reduce_z():
        for g in range(2):
            take(g2_r.at[g, pl.ds(0, 15)], G2 + g)
            total = g_own[g, chunk]
            for c in range(16):
                total = total + g2_r[g, c].astype(F32)
            g_sum[g] = total.reshape(4, 8, WIDTH)
        for i in range(4):
            zz = core * 8 + yh * 4 + i
            g3_s[i] = jnp.concatenate([g_sum[0, i], g_sum[1, i]], 0).astype(BF16)

            @pl.when(zz != z)
            def _():
                send(g3_s.at[i], g3_r.at[z], G3, at_p(yl * 16 + zz))

    owner = (lax.div(z, 8) == core) & (lax.rem(lax.div(z, 4), 2) == yh)

    def reduce_last():
        @pl.when(owner)
        def _():
            take(g3_r.at[pl.ds(0, NZ - 1)], G3)
            g3_r[z] = g3_s[lax.rem(z, 4)]
            total = g3_r[0].astype(F32)
            for i in range(1, NZ):
                total = total + g3_r[i].astype(F32)
            g4_s[...] = total
            for c in (1, 2, 3):
                send(g4_s, g4_r, G4, (ring(dp, c, 4), ctx))

    def finish():
        @pl.when(owner)
        def _():
            g4_r[...] = g4_s[...]

        @pl.when(jnp.logical_not(owner))
        def _():
            take(g4_r, G4)

        gw_ref[:, :WIDTH] = g4_r[0:6, :]
        gw_ref[:, WIDTH:] = g4_r[8:14, :]

    load_unpad.wait()
    take(rt_r.at[pl.ds(0, 3)], RT)
    for index, ref in enumerate((att_ref, gq_ref, gk_ref, gv_ref)):
        heads = jnp.concatenate([rt_r[h, index] for h in range(HEADS)], axis=1)
        ref[:, :WIDTH] = dot(heads, unpad_ref[...]).astype(BF16)
    reduce_core(0)
    reduce_plane(0)
    unpack(3, [((att_ref, WIDTH), (gq_ref, WIDTH))])
    unpack(4, [((att_ref, WIDTH + 128), (att_ref, WIDTH + 256))])
    reduce_core(1)
    exchange(6)
    exchange(7)
    reduce_plane(1)
    reduce_z()
    exchange(8)
    unpack(5, [((gk_ref, WIDTH), (gv_ref, WIDTH))])
    unpack(6, [((gq_ref, WIDTH + 128), (gq_ref, WIDTH + 256))])
    stores[0].start()
    unpack(7, [((gk_ref, WIDTH + 128), (gk_ref, WIDTH + 256))])
    stores[1].start()
    reduce_last()
    unpack(8, [((gv_ref, WIDTH + 128), (gv_ref, WIDTH + 256))])
    stores[2].start()
    finish()
    stores[3].start()

    for slot in range(9):
        sent(cs[slot].at[pl.ds(0, GROUP - 1)], slot)
    sent(wz_recv.at[pl.ds(0, NZ - 1)], WZ)
    sent(rs.at[pl.ds(0, 3)], RQ)
    sent(wg.at[core, pl.ds(0, 15)], WX)
    sent(wg.at[core], WC)
    sent(rs_do.at[pl.ds(0, 3)], RD)
    sent(rt_s.at[pl.ds(0, 3)], RT)
    for g in range(2):
        sent(g1_s.at[g], G1 + g)
        sent(g2_s.at[g, pl.ds(0, 15)], G2 + g)

    @pl.when(owner)
    def _():
        sent(g3_s.at[pl.ds(0, 3)], G3)
        sent(g_sum.at[pl.ds(0, 2), pl.ds(0, 3)], G4)

    @pl.when(jnp.logical_not(owner))
    def _():
        sent(g3_s, G3)
    for store in stores:
        store.wait()


def hand_over(*refs):
    n = 4
    srcs, dsts, held, sems = refs[:n], refs[n : 2 * n], refs[2 * n : 3 * n], refs[3 * n]
    inward, outward = [], []
    for src, dst, mid in zip(srcs, dsts, held, strict=True):
        half = ROWS // 2
        pieces = (pl.ds(0, half), pl.ds(half, half)) if src.shape[0] == ROWS else (pl.ds(0, src.shape[0]),)
        for piece in pieces:
            i = len(inward)
            inward.append(pltpu.make_async_copy(src.at[piece], mid.at[piece], sems.at[0, i]))
            outward.append(pltpu.make_async_copy(mid.at[piece], dst.at[piece], sems.at[1, i]))
    for copy in inward:
        copy.start()
    for first, second in zip(inward, outward, strict=True):
        first.wait()
        second.start()
    for copy in outward:
        copy.wait()


def body(queries, key_rows, value_rows, out_weight, cotangent, *matrices):
    hbm = pl.BlockSpec(memory_space=pltpu.HBM)
    tokens = jax.ShapeDtypeStruct((ROWS, 2 * WIDTH), BF16)
    weight = jax.ShapeDtypeStruct((6, 2 * WIDTH), F32)
    inputs = (queries[0], key_rows[0], value_rows[0], out_weight, cotangent[0], *matrices)
    messages = [pltpu.VMEM((GROUP, 16, 128 * t), BF16) for t in TILES]
    outs = pl.pallas_call(
        kernel,
        out_shape=(tokens, tokens, tokens, weight),
        in_specs=[hbm] * len(inputs),
        out_specs=(hbm,) * 4,
        scratch_shapes=[pltpu.VMEM(a.shape, a.dtype) for a in inputs]
        + [
            pltpu.VMEM((16, 128), F32),
            pltpu.VMEM((16, 128), BF16),
            pltpu.VMEM((NZ, 16, 128), BF16),
            pltpu.VMEM((2, 16, 48, WIDTH), BF16),
            pltpu.VMEM((ROWS, 768), BF16),
            pltpu.VMEM((1024, ROWS), BF16),
            pltpu.VMEM((ROWS, 2 * WIDTH), BF16),
            *messages,
            *messages,
            pltpu.VMEM((ROWS, WIDTH), BF16),
            pltpu.VMEM((ROWS, WIDTH), BF16),
            pltpu.VMEM((ROWS, WIDTH), BF16),
            pltpu.VMEM((ROWS, WIDTH), BF16),
            pltpu.VMEM((HEADS, ROWS, ROWS), F32),
            pltpu.VMEM((HEADS, ROWS, ROWS), BF16),
            pltpu.VMEM((HEADS, ROWS, ROWS), BF16),
            pltpu.VMEM((ROWS, WIDTH), F32),
            pltpu.VMEM((ROWS, WIDTH), F32),
            pltpu.VMEM((ROWS, WIDTH), F32),
            pltpu.VMEM((ROWS, WIDTH), F32),
            pltpu.VMEM((4, 3, ROWS, 128), BF16),
            pltpu.VMEM((4, 3, ROWS, 128), BF16),
            pltpu.VMEM((4, ROWS, 128), BF16),
            pltpu.VMEM((4, ROWS, 128), BF16),
            pltpu.VMEM((4, 4, ROWS, 128), BF16),
            pltpu.VMEM((4, 4, ROWS, 128), BF16),
            pltpu.VMEM((1024, 128), F32),
            pltpu.VMEM((1024, 128), F32),
            pltpu.VMEM((ROWS, 2 * WIDTH), BF16),
            pltpu.VMEM((2, 512, WIDTH), BF16),
            pltpu.VMEM((2, 512, WIDTH), BF16),
            pltpu.VMEM((2, 16, 32, WIDTH), F32),
            pltpu.VMEM((2, 16, 32, WIDTH), BF16),
            pltpu.VMEM((2, 16, 32, WIDTH), BF16),
            pltpu.VMEM((2, 4, 8, WIDTH), F32),
            pltpu.VMEM((4, 16, WIDTH), BF16),
            pltpu.VMEM((NZ, 16, WIDTH), BF16),
            pltpu.VMEM((16, WIDTH), F32),
            pltpu.VMEM((16, WIDTH), F32),
            pltpu.VMEM(tokens.shape, BF16),
            pltpu.VMEM(tokens.shape, BF16),
            pltpu.VMEM(tokens.shape, BF16),
            pltpu.VMEM(weight.shape, F32),
            pltpu.SemaphoreType.DMA((4,)),
            pltpu.SemaphoreType.DMA((len(inputs),)),
            pltpu.SemaphoreType.DMA((SEMS,)),
            pltpu.SemaphoreType.DMA((SEMS,)),
        ],
        compiler_params=pltpu.CompilerParams(
            collective_id=0, has_side_effects=True, vmem_limit_bytes=60 * 1024 * 1024
        ),
        cost_estimate=pl.CostEstimate(
            flops=8_000_000_000, bytes_accessed=8_000_000, transcendentals=2_000_000
        ),
        name="strided_attention",
    )(*inputs)
    outs = pl.pallas_call(
        hand_over,
        out_shape=(tokens, tokens, tokens, weight),
        in_specs=[hbm] * 4,
        out_specs=(hbm,) * 4,
        scratch_shapes=[pltpu.VMEM(a.shape, a.dtype) for a in outs] + [pltpu.SemaphoreType.DMA((2, 7))],
        name="hand_over",
    )(*outs)
    return (outs[0][None], outs[1][None], outs[2][None], outs[3])


def solution(mesh):
    tokens, rows = P("dp", "ctx", None), P("ctx", None)
    matrices = selections()
    mapped = jax.shard_map(
        body,
        mesh=mesh,
        in_specs=(tokens, tokens, tokens, rows, tokens) + (P(None, None),) * len(matrices),
        out_specs=(tokens, tokens, tokens, rows),
        check_vma=False,
    )

    def run(queries, key_rows, value_rows, out_weight, cotangent):
        return mapped(queries, key_rows, value_rows, out_weight, cotangent, *matrices)

    return run
```

```python
import jax
import jax.numpy as jnp
import numpy as np
from jax import lax
from jax.experimental import pallas as pl
from jax.experimental.pallas import tpu as pltpu
from jax.sharding import PartitionSpec as P

HS = 96
HEADS = 4
WIDTH = HEADS * HS
NX, NZ = 4, 16
GROUP = 32
ROWS = 256
CLASSES = 8
SCALE = HS**-0.5
F32, BF16 = jnp.float32, jnp.bfloat16
NT = (((1,), (1,)), ((), ()))
TN = (((0,), (0,)), ((), ()))


def dot(a, b, dims=None):
    if dims is None:
        return jnp.dot(a, b, preferred_element_type=F32)
    return lax.dot_general(a, b, dims, preferred_element_type=F32)


def selections():
    spread = np.zeros((768, 768), np.float32)
    gather = np.zeros((1024, 768), np.float32)
    for yl in range(2):
        for z in range(NZ):
            for x in range(NX):
                for r in range(6):
                    f = (yl * 64 + z * 4 + x) * 6 + r
                    spread[f, (((r // 3 * 2 + yl) * 4 + x) * 16 + z) * 3 + r % 3] = 1
                    gather[(((z // 8 * 4 + x) * 2 + yl) * 8 + z % 8) * 8 + r, f] = 1
    rows = np.zeros((3, 48, 256), np.float32)
    for t in range(3):
        for z in range(NZ):
            for r in range(3):
                rows[t, z * 3 + r, z * 16 + r * 3 + t] = 1
    pad = np.zeros((WIDTH, 512), np.float32)
    for h in range(HEADS):
        for i in range(HS):
            pad[h * HS + i, h * 128 + i] = 1
    return [jnp.asarray(m, BF16) for m in (spread, gather, rows, pad, pad.T)]


WZ, WX, WC, RQ, RD, RT, G1, G2, G3, G4 = 9, 10, 11, 12, 13, 14, 15, 17, 19, 20
SEMS = 21
TILES = (4, 1, 1, 1, 1, 1, 1, 1, 1)
EARLY_PLANES, LATE_PLANES = (0, 1, 2, 3), (4, 15, 5, 14, 6, 13, 7, 12, 8, 9, 10, 11)


def kernel(
    q_hbm, k_hbm, v_hbm, w_hbm, c_hbm, spread_hbm, gather_hbm, rows_hbm, pad_hbm, unpad_hbm,
    gq_hbm, gk_hbm, gv_hbm, gw_hbm,
    q_ref, k_ref, v_ref, w_ref, c_ref, spread_ref, gather_ref, rows_ref, pad_ref, unpad_ref,
    wz_rows, wz_send, wz_recv, wg, cot_p, cot_t, go,
    cs0, cs1, cs2, cs3, cs4, cs5, cs6, cs7, cs8, cr0, cr1, cr2, cr3, cr4, cr5, cr6, cr7, cr8,
    qc, kc, vc, dc, probs_ref, half_ref, ds_ref, att_a, dq_a, dk_a, dv_a,
    rs, rr, rs_do, rr_do, rt_s, rt_r, racc_k, racc_v, att_ref,
    g1_s, g1_r, g_own, g2_s, g2_r, g_sum, g3_s, g3_r, g4_s, g4_r,
    gq_ref, gk_ref, gv_ref, gw_ref, osem, isem, ssem, rsem,
):
    cs = (cs0, cs1, cs2, cs3, cs4, cs5, cs6, cs7, cs8)
    cr = (cr0, cr1, cr2, cr3, cr4, cr5, cr6, cr7, cr8)
    dp, ctx = lax.axis_index("dp"), lax.axis_index("ctx")
    core, yh = lax.rem(dp, 2), lax.div(dp, 2)
    x, p = lax.rem(ctx, 4), lax.div(ctx, 4)
    z, yl = lax.rem(p, 16), lax.div(p, 16)
    y = yh * 2 + yl
    chunk = x * 4 + yl * 2 + yh

    loads = [
        pltpu.make_async_copy(src, dst, isem.at[i])
        for i, (src, dst) in enumerate(
            (
                (q_hbm, q_ref), (k_hbm, k_ref), (v_hbm, v_ref), (w_hbm, w_ref), (pad_hbm, pad_ref),
                (c_hbm, c_ref), (spread_hbm, spread_ref), (rows_hbm, rows_ref),
                (gather_hbm, gather_ref), (unpad_hbm, unpad_ref),
            )
        )
    ]
    (load_q, load_k, load_v, load_w, load_pad, load_c, load_spread, load_rows, load_gather,
     load_unpad) = loads
    for load in loads[:4]:
        load.start()

    stores = [
        pltpu.make_async_copy(src, dst, osem.at[i])
        for i, (src, dst) in enumerate(
            ((gq_ref, gq_hbm), (gk_ref, gk_hbm), (gv_ref, gv_hbm), (gw_ref, gw_hbm))
        )
    ]

    def at_p(pp):
        return (dp, pp * 4 + x)

    def at_x(xx):
        return (dp, p * 4 + xx)

    def at_y(yy):
        return (lax.div(yy, 2) * 2 + core, lax.rem(yy, 2) * 64 + z * 4 + x)

    def at_chunk(c):
        return (lax.rem(c, 2) * 2 + core, lax.rem(lax.div(c, 2), 2) * 64 + z * 4 + lax.div(c, 4))

    def at_core():
        return (yh * 2 + 1 - core, ctx)

    def ring(i, by, n):
        return lax.rem(i + by, n)

    def send(src, dst, sem, where):
        pltpu.make_async_remote_copy(
            src_ref=src, dst_ref=dst, send_sem=ssem.at[sem], recv_sem=rsem.at[sem],
            device_id=where, device_id_type=pl.DeviceIdType.MESH,
        ).start()

    def take(ref, sem):
        pltpu.make_async_copy(ref, ref, rsem.at[sem]).wait()

    def sent(ref, sem):
        pltpu.make_async_copy(ref, ref, ssem.at[sem]).wait()

    barrier = pltpu.get_barrier_semaphore()

    def greet(where):
        pl.semaphore_signal(barrier, inc=1, device_id=where, device_id_type=pl.DeviceIdType.MESH)

    def greet_p(i, _):
        greet(at_p(ring(p, i, GROUP)))
        return 0

    lax.fori_loop(1, GROUP, greet_p, 0)


    def greet_chunk(i, _):
        greet(at_chunk(ring(chunk, i, 16)))
        return 0

    lax.fori_loop(1, 16, greet_chunk, 0)
    greet(at_core())
    greet(((1 - yh) * 2 + 1 - core, ctx))
    for load in loads[4:]:
        load.start()

    def pack(slot, pairs):
        def one(m, _):
            rows = pl.ds(pl.multiple_of(m * 16, 16), 16)
            for t, ((a_ref, a0), (b_ref, b0)) in enumerate(pairs):
                a = a_ref[rows, a0 : a0 + 128].astype(F32)
                b = b_ref[rows, b0 : b0 + 128].astype(F32)
                lanes = slice(t * 128, (t + 1) * 128)
                cs[slot][2 * m, :, lanes] = jnp.concatenate([a[:8], b[:8]], 0).astype(BF16)
                cs[slot][2 * m + 1, :, lanes] = jnp.concatenate([a[8:], b[8:]], 0).astype(BF16)
            return 0

        lax.fori_loop(0, 16, one, 0)

    def exchange(slot, planes=None):
        def one(i, _):
            half = lax.div(i + 1, 2)
            odd = lax.rem(i, 2)
            pp = ring(p, odd * half + (1 - odd) * (GROUP - half), GROUP)
            send(cs[slot].at[pp], cr[slot].at[p], slot, at_p(pp))
            return 0

        if planes is None:
            lax.fori_loop(1, GROUP, one, 0)
        else:
            for zz in planes:
                for by in range(2):
                    pp = ring(yl, by, 2) * 16 + zz

                    @pl.when(pp != p)
                    def _():
                        send(cs[slot].at[pp], cr[slot].at[p], slot, at_p(pp))

        if planes is not LATE_PLANES:
            cr[slot][p] = cs[slot][p]

    def unpack(slot, pairs):
        take(cr[slot].at[pl.ds(0, GROUP - 1)], slot)

        def one(m, _):
            rows = pl.ds(pl.multiple_of(m * 16, 16), 16)
            for t, ((a_ref, a0), (b_ref, b0)) in enumerate(pairs):
                lanes = slice(t * 128, (t + 1) * 128)
                first = cr[slot][2 * m, :, lanes].astype(F32)
                second = cr[slot][2 * m + 1, :, lanes].astype(F32)
                a_ref[rows, a0 : a0 + 128] = jnp.concatenate([first[:8], second[:8]], 0).astype(BF16)
                b_ref[rows, b0 : b0 + 128] = jnp.concatenate([first[8:], second[8:]], 0).astype(BF16)
            return 0

        lax.fori_loop(0, 16, one, 0)

    load_q.wait()
    load_k.wait()
    load_v.wait()
    pack(
        0,
        [((q_ref, WIDTH + t), (k_ref, WIDTH + t)) for t in (0, 128, 256)]
        + [((v_ref, WIDTH), (v_ref, WIDTH + 128))],
    )
    load_w.wait()
    w = w_ref[...].astype(F32)
    w = jnp.where(core == 0, w[:, :WIDTH], w[:, WIDTH:])
    w = jnp.where(yh == 0, w[0:3], w[3:6])
    wz_rows[...] = jnp.zeros((16, 128), F32)
    for r in range(3):
        for t in range(3):
            wz_rows[r * 3 + t : r * 3 + t + 1, :] = w[r : r + 1, t * 128 : (t + 1) * 128]
    wz_send[...] = wz_rows[...].astype(BF16)
    wz_recv[z] = wz_send[...]
    pl.semaphore_wait(barrier, 48)

    def send_w(i, _):
        send(wz_send, wz_recv.at[z], WZ, at_p(yl * 16 + ring(z, i, NZ)))
        return 0

    lax.fori_loop(1, NZ, send_w, 0)
    exchange(0)

    load_pad.wait()
    for index, ref in enumerate((q_ref, k_ref, v_ref)):
        padded = dot(ref[:, :WIDTH], pad_ref[...]).astype(BF16)
        for h in range(HEADS):
            rs[h, index] = padded[:, h * 128 : (h + 1) * 128]
    for i in range(1, 4):
        xx = ring(x, i, 4)
        send(rs.at[xx], rr.at[x], RQ, at_x(xx))
    rr[x] = rs[x]

    load_rows.wait()
    take(wz_recv.at[pl.ds(0, NZ - 1)], WZ)
    at = yh * 8 + yl * 4 + x
    gathered = wz_recv[...].reshape(256, 128)
    for t in range(3):
        wg[core, at, :, t * 128 : (t + 1) * 128] = dot(rows_ref[t], gathered).astype(BF16)
    own = wg.at[core, at]

    def send_plane(i, _):
        send(own, own, WX, at_chunk(ring(chunk, i, 16)))
        return 0

    lax.fori_loop(1, 16, send_plane, 0)

    load_c.wait()
    load_spread.wait()
    cot_p[...] = dot(c_ref[...], spread_ref[...]).astype(BF16)

    load_gather.wait()
    cot_t[...] = dot(gather_ref[...], c_ref[...], NT).astype(BF16)
    take(wg.at[core, pl.ds(0, 15)], WX)
    send(wg.at[core], wg.at[core], WC, at_core())
    take(wg.at[1 - core], WC)

    def grad_out(c):
        go[:, c * WIDTH : (c + 1) * WIDTH] = dot(
            cot_p[...], wg[c].reshape(768, WIDTH)
        ).astype(BF16)

    grad_out(1)
    pack(1, [((go, WIDTH), (go, WIDTH + 128))])
    exchange(1)
    pack(2, [((go, WIDTH + 256), (v_ref, WIDTH + 256))])
    exchange(2)
    grad_out(0)
    padded = dot(go[:, :WIDTH], pad_ref[...]).astype(BF16)
    for h in range(HEADS):
        rs_do[h] = padded[:, h * 128 : (h + 1) * 128]
    for i in range(1, 4):
        xx = ring(x, i, 4)
        send(rs_do.at[xx], rr_do.at[x], RD, at_x(xx))
    rr_do[x] = rs_do[x]

    unpack(0, [((qc, t), (kc, t)) for t in (0, 128, 256)] + [((vc, 0), (vc, 128))])
    row_at = lax.broadcasted_iota(jnp.int32, (ROWS, ROWS), 0)
    key_at = lax.broadcasted_iota(jnp.int32, (ROWS, ROWS), 1)
    lanes = lax.broadcasted_iota(jnp.int32, (ROWS, WIDTH), 1)

    def span(h):
        return h * HS // 128 * 128, -(-(h + 1) * HS // 128) * 128

    def head(ref, h):
        lo, hi = span(h)
        at = lanes[:, lo:hi]
        value = ref[:, lo:hi]
        return jnp.where((at >= h * HS) & (at < (h + 1) * HS), value, jnp.zeros_like(value))

    def put(ref, h, value):
        lo, hi = span(h)
        for t in range(lo, hi, 128):
            if h > 0 and t == lo:
                ref[:, t : t + 128] += value[:, t - lo : t - lo + 128]
            else:
                ref[:, t : t + 128] = value[:, t - lo : t - lo + 128]

    def softmax(scores):
        top = jnp.max(scores, axis=1, keepdims=True)
        total = top + jnp.log(jnp.sum(jnp.exp(scores - top), axis=1, keepdims=True))
        return jnp.exp(scores - total)

    for h in range(HEADS):
        lo, hi = span(h)
        scores = dot(head(qc, h), kc[:, lo:hi], NT) * SCALE
        allowed = (key_at <= row_at) & (lax.rem(row_at - key_at, CLASSES) == 0)
        probs = softmax(jnp.where(allowed, scores, -1e30))
        probs_ref[h] = probs
        half_ref[h] = probs.astype(BF16)

    take(rr.at[pl.ds(0, 3)], RQ)
    take(rr_do.at[pl.ds(0, 3)], RD)
    racc_k[...] = jnp.zeros_like(racc_k)
    racc_v[...] = jnp.zeros_like(racc_v)
    for i in range(4):
        n = (i + 1) * ROWS
        query, out = rr[i, 0], rr_do[i]
        keys = rr[0 : i + 1, 1].reshape(n, 128)
        values = rr[0 : i + 1, 2].reshape(n, 128)
        at = lax.broadcasted_iota(jnp.int32, (ROWS, n), 0) + i * ROWS
        allowed = lax.broadcasted_iota(jnp.int32, (ROWS, n), 1) <= at
        probs = softmax(jnp.where(allowed, dot(query, keys, NT) * SCALE, -1e30))
        half = probs.astype(BF16)
        attended = dot(half, values).astype(BF16)
        deltas = jnp.sum(out.astype(F32) * attended.astype(F32), axis=1, keepdims=True)
        dscores = (probs * (dot(out, values, NT) - deltas) * SCALE).astype(BF16)
        rt_s[i, 0] = attended
        rt_s[i, 1] = dot(dscores, keys).astype(BF16)
        racc_k[0:n, :] += dot(dscores, query, TN)
        racc_v[0:n, :] += dot(half, out, TN)
    for i in range(4):
        rt_s[i, 2] = racc_k[i * ROWS : (i + 1) * ROWS, :].astype(BF16)
        rt_s[i, 3] = racc_v[i * ROWS : (i + 1) * ROWS, :].astype(BF16)
    for i in range(1, 4):
        xx = ring(x, i, 4)
        send(rt_s.at[xx], rt_r.at[x], RT, at_x(xx))
    rt_r[x] = rt_s[x]

    def attend(h):
        put(att_a, h, dot(half_ref[h], head(vc, h)).astype(BF16).astype(F32))

    def score_grads(h):
        lo, hi = span(h)
        out = head(dc, h)
        deltas = jnp.sum(out.astype(F32) * att_a[:, lo:hi], axis=1, keepdims=True)
        dprobs = dot(out, vc[:, lo:hi], NT)
        dscores = (probs_ref[h] * (dprobs - deltas) * SCALE).astype(BF16)
        ds_ref[h] = dscores
        put(dq_a, h, dot(dscores, head(kc, h)))

    def key_grads(h):
        put(dk_a, h, dot(ds_ref[h], head(qc, h), TN))
        put(dv_a, h, dot(half_ref[h], head(dc, h), TN))

    unpack(1, [((dc, 0), (dc, 128))])
    for h in (0, 1):
        attend(h)
        score_grads(h)
    pack(3, [((att_a, 0), (dq_a, 0))])
    exchange(3)
    for h in (0, 1):
        key_grads(h)
    unpack(2, [((dc, 256), (vc, 256))])
    for h in (2, 3):
        attend(h)
    pack(4, [((att_a, 128), (att_a, 256))])
    exchange(4)
    pack(5, [((dk_a, 0), (dv_a, 0))])
    exchange(5)
    for h in (2, 3):
        score_grads(h)
        key_grads(h)
    pack(6, [((dq_a, 128), (dq_a, 256))])
    pack(7, [((dk_a, 128), (dk_a, 256))])
    pack(8, [((dv_a, 128), (dv_a, 256))])

    def reduce_core(g):
        attended = att_ref[:, g * WIDTH : (g + 1) * WIDTH]
        theirs = pl.ds(pl.multiple_of((1 - core) * 512, 512), 512)
        ours = pl.ds(pl.multiple_of(core * 512, 512), 512)
        g1_s[g] = dot(cot_t[theirs, :], attended).astype(BF16)
        send(g1_s.at[g], g1_r.at[g], G1 + g, at_core())
        g_own[g] = dot(cot_t[ours, :], attended).reshape(16, 32, WIDTH)

    def reduce_plane(g):
        take(g1_r.at[g], G1 + g)
        total = g_own[g] + g1_r[g].astype(F32).reshape(16, 32, WIDTH)
        g_own[g] = total
        g2_s[g] = total.astype(BF16)

        def one(i, _):
            c = ring(chunk, i, 16)
            send(g2_s.at[g, c], g2_r.at[g, chunk], G2 + g, at_chunk(c))
            return 0

        lax.fori_loop(1, 16, one, 0)
        g2_r[g, chunk] = jnp.zeros((32, WIDTH), BF16)

    def reduce_z():
        for g in range(2):
            take(g2_r.at[g, pl.ds(0, 15)], G2 + g)
            total = g_own[g, chunk]
            for c in range(16):
                total = total + g2_r[g, c].astype(F32)
            g_sum[g] = total.reshape(4, 8, WIDTH)
        for i in range(4):
            zz = core * 8 + yh * 4 + i
            g3_s[i] = jnp.concatenate([g_sum[0, i], g_sum[1, i]], 0).astype(BF16)

            @pl.when(zz != z)
            def _():
                send(g3_s.at[i], g3_r.at[z], G3, at_p(yl * 16 + zz))

    owner = (lax.div(z, 8) == core) & (lax.rem(lax.div(z, 4), 2) == yh)

    def reduce_last():
        @pl.when(owner)
        def _():
            take(g3_r.at[pl.ds(0, NZ - 1)], G3)
            g3_r[z] = g3_s[lax.rem(z, 4)]
            total = g3_r[0].astype(F32)
            for i in range(1, NZ):
                total = total + g3_r[i].astype(F32)
            g4_s[...] = total
            for c in (1, 2, 3):
                send(g4_s, g4_r, G4, (ring(dp, c, 4), ctx))

    def finish():
        @pl.when(owner)
        def _():
            g4_r[...] = g4_s[...]

        @pl.when(jnp.logical_not(owner))
        def _():
            take(g4_r, G4)

        gw_ref[:, :WIDTH] = g4_r[0:6, :]
        gw_ref[:, WIDTH:] = g4_r[8:14, :]

    load_unpad.wait()
    take(rt_r.at[pl.ds(0, 3)], RT)
    for index, ref in enumerate((att_ref, gq_ref, gk_ref, gv_ref)):
        heads = jnp.concatenate([rt_r[h, index] for h in range(HEADS)], axis=1)
        ref[:, :WIDTH] = dot(heads, unpad_ref[...]).astype(BF16)
    reduce_core(0)
    reduce_plane(0)
    unpack(3, [((att_ref, WIDTH), (gq_ref, WIDTH))])
    unpack(4, [((att_ref, WIDTH + 128), (att_ref, WIDTH + 256))])
    reduce_core(1)
    for slot in (6, 7, 8):
        exchange(slot, EARLY_PLANES)
    for slot in (6, 7):
        exchange(slot, LATE_PLANES)
    reduce_plane(1)
    reduce_z()
    exchange(8, LATE_PLANES)
    unpack(5, [((gk_ref, WIDTH), (gv_ref, WIDTH))])
    unpack(6, [((gq_ref, WIDTH + 128), (gq_ref, WIDTH + 256))])
    stores[0].start()
    unpack(7, [((gk_ref, WIDTH + 128), (gk_ref, WIDTH + 256))])
    stores[1].start()
    reduce_last()
    unpack(8, [((gv_ref, WIDTH + 128), (gv_ref, WIDTH + 256))])
    stores[2].start()
    finish()
    stores[3].start()

    for slot in range(9):
        sent(cs[slot].at[pl.ds(0, GROUP - 1)], slot)
    sent(wz_recv.at[pl.ds(0, NZ - 1)], WZ)
    sent(rs.at[pl.ds(0, 3)], RQ)
    sent(wg.at[core, pl.ds(0, 15)], WX)
    sent(wg.at[core], WC)
    sent(rs_do.at[pl.ds(0, 3)], RD)
    sent(rt_s.at[pl.ds(0, 3)], RT)
    for g in range(2):
        sent(g1_s.at[g], G1 + g)
        sent(g2_s.at[g, pl.ds(0, 15)], G2 + g)

    @pl.when(owner)
    def _():
        sent(g3_s.at[pl.ds(0, 3)], G3)
        sent(g_sum.at[pl.ds(0, 2), pl.ds(0, 3)], G4)

    @pl.when(jnp.logical_not(owner))
    def _():
        sent(g3_s, G3)
    for store in stores:
        store.wait()


def hand_over(*refs):
    n = 4
    srcs, dsts, held, sems = refs[:n], refs[n : 2 * n], refs[2 * n : 3 * n], refs[3 * n]
    inward, outward = [], []
    for src, dst, mid in zip(srcs, dsts, held, strict=True):
        half = ROWS // 2
        pieces = (pl.ds(0, half), pl.ds(half, half)) if src.shape[0] == ROWS else (pl.ds(0, src.shape[0]),)
        for piece in pieces:
            i = len(inward)
            inward.append(pltpu.make_async_copy(src.at[piece], mid.at[piece], sems.at[0, i]))
            outward.append(pltpu.make_async_copy(mid.at[piece], dst.at[piece], sems.at[1, i]))
    for copy in inward:
        copy.start()
    for first, second in zip(inward, outward, strict=True):
        first.wait()
        second.start()
    for copy in outward:
        copy.wait()


def body(queries, key_rows, value_rows, out_weight, cotangent, *matrices):
    hbm = pl.BlockSpec(memory_space=pltpu.HBM)
    tokens = jax.ShapeDtypeStruct((ROWS, 2 * WIDTH), BF16)
    weight = jax.ShapeDtypeStruct((6, 2 * WIDTH), F32)
    inputs = (queries[0], key_rows[0], value_rows[0], out_weight, cotangent[0], *matrices)
    messages = [pltpu.VMEM((GROUP, 16, 128 * t), BF16) for t in TILES]
    outs = pl.pallas_call(
        kernel,
        out_shape=(tokens, tokens, tokens, weight),
        in_specs=[hbm] * len(inputs),
        out_specs=(hbm,) * 4,
        scratch_shapes=[pltpu.VMEM(a.shape, a.dtype) for a in inputs]
        + [
            pltpu.VMEM((16, 128), F32),
            pltpu.VMEM((16, 128), BF16),
            pltpu.VMEM((NZ, 16, 128), BF16),
            pltpu.VMEM((2, 16, 48, WIDTH), BF16),
            pltpu.VMEM((ROWS, 768), BF16),
            pltpu.VMEM((1024, ROWS), BF16),
            pltpu.VMEM((ROWS, 2 * WIDTH), BF16),
            *messages,
            *messages,
            pltpu.VMEM((ROWS, WIDTH), BF16),
            pltpu.VMEM((ROWS, WIDTH), BF16),
            pltpu.VMEM((ROWS, WIDTH), BF16),
            pltpu.VMEM((ROWS, WIDTH), BF16),
            pltpu.VMEM((HEADS, ROWS, ROWS), F32),
            pltpu.VMEM((HEADS, ROWS, ROWS), BF16),
            pltpu.VMEM((HEADS, ROWS, ROWS), BF16),
            pltpu.VMEM((ROWS, WIDTH), F32),
            pltpu.VMEM((ROWS, WIDTH), F32),
            pltpu.VMEM((ROWS, WIDTH), F32),
            pltpu.VMEM((ROWS, WIDTH), F32),
            pltpu.VMEM((4, 3, ROWS, 128), BF16),
            pltpu.VMEM((4, 3, ROWS, 128), BF16),
            pltpu.VMEM((4, ROWS, 128), BF16),
            pltpu.VMEM((4, ROWS, 128), BF16),
            pltpu.VMEM((4, 4, ROWS, 128), BF16),
            pltpu.VMEM((4, 4, ROWS, 128), BF16),
            pltpu.VMEM((1024, 128), F32),
            pltpu.VMEM((1024, 128), F32),
            pltpu.VMEM((ROWS, 2 * WIDTH), BF16),
            pltpu.VMEM((2, 512, WIDTH), BF16),
            pltpu.VMEM((2, 512, WIDTH), BF16),
            pltpu.VMEM((2, 16, 32, WIDTH), F32),
            pltpu.VMEM((2, 16, 32, WIDTH), BF16),
            pltpu.VMEM((2, 16, 32, WIDTH), BF16),
            pltpu.VMEM((2, 4, 8, WIDTH), F32),
            pltpu.VMEM((4, 16, WIDTH), BF16),
            pltpu.VMEM((NZ, 16, WIDTH), BF16),
            pltpu.VMEM((16, WIDTH), F32),
            pltpu.VMEM((16, WIDTH), F32),
            pltpu.VMEM(tokens.shape, BF16),
            pltpu.VMEM(tokens.shape, BF16),
            pltpu.VMEM(tokens.shape, BF16),
            pltpu.VMEM(weight.shape, F32),
            pltpu.SemaphoreType.DMA((4,)),
            pltpu.SemaphoreType.DMA((len(inputs),)),
            pltpu.SemaphoreType.DMA((SEMS,)),
            pltpu.SemaphoreType.DMA((SEMS,)),
        ],
        compiler_params=pltpu.CompilerParams(
            collective_id=0, has_side_effects=True, vmem_limit_bytes=60 * 1024 * 1024
        ),
        cost_estimate=pl.CostEstimate(
            flops=8_000_000_000, bytes_accessed=8_000_000, transcendentals=2_000_000
        ),
        name="strided_attention",
    )(*inputs)
    outs = pl.pallas_call(
        hand_over,
        out_shape=(tokens, tokens, tokens, weight),
        in_specs=[hbm] * 4,
        out_specs=(hbm,) * 4,
        scratch_shapes=[pltpu.VMEM(a.shape, a.dtype) for a in outs] + [pltpu.SemaphoreType.DMA((2, 7))],
        name="hand_over",
    )(*outs)
    return (outs[0][None], outs[1][None], outs[2][None], outs[3])


def solution(mesh):
    tokens, rows = P("dp", "ctx", None), P("ctx", None)
    matrices = selections()
    mapped = jax.shard_map(
        body,
        mesh=mesh,
        in_specs=(tokens, tokens, tokens, rows, tokens) + (P(None, None),) * len(matrices),
        out_specs=(tokens, tokens, tokens, rows),
        check_vma=False,
    )

    def run(queries, key_rows, value_rows, out_weight, cotangent):
        return mapped(queries, key_rows, value_rows, out_weight, cotangent, *matrices)

    return run
```
